512 devices in a mesh: dp: 4 (over y), tenant: 8 (over x, core), mp: 16 (over z).
Axes of the slice: x: 4, y: 4, z: 16, core: 2. Of those that a mesh axis runs over, the one named last changes fastest.
Arguments:
- cross_in: bfloat16 [32768, 3456], P(('dp', 'tenant'), 'mp'), may hold values from -6 to 6
- rank_act: bfloat16 [32768, 512], P(('dp', 'tenant')), may hold values from -6 to 6
- tower_cot: bfloat16 [32768, 1024], P(('dp', 'tenant')), may hold values from -6 to 6
- tenant_ids: int32 [32768, 1], P(('dp', 'tenant')), may hold values from 0 to 31; in each aligned block of 1024 rows (0 to 1023, 1024 to 2047, ...) at most 40 rows name the same one
- sparse_ids: int32 [32768, 26], P(('dp', 'tenant')), may hold values from 0 to 1023
- table_slot: int32 [26], replicated, may hold values from 0 to 31, as said below
- cross_u: bfloat16 [3456, 512], P('mp'), may hold values from -0.25 to 0.25
- cross_v: bfloat16 [3456, 512], P('mp'), may hold values from -0.109375 to 0.109375
- cross_bias: float32 [3456], P('mp'), may hold values from -1 to 1
- tower_w: bfloat16 [32, 3456, 1024], P(('dp', 'tenant'), 'mp'), may hold values from -0.1875 to 0.1875
Outputs:
- tower_wgrad: bfloat16 [32, 3456, 1024], P(('dp', 'tenant'), 'mp')
- cross_ugrad: float32 [3456, 512], P('mp')
- cross_vgrad: float32 [3456, 512], P('mp')
- cross_bgrad: float32 [3456], P('mp')
- table_grad: bfloat16 [32, 32, 1024, 128], P(('dp', 'tenant'), 'mp')
The draws below stay inside these ranges and needn't reach their ends.
Inputs may be any that keep to these rules, and one draw needn't show every extreme that they name: `tenant_ids`: in each aligned block of 1024 rows (one sample group) no tenant is named more than 40 times, a bound that some block reaches. `table_slot`: distinct slots for distinct tables.
All inputs are finite; a program needn't handle non-finite values.
Results may differ from the reference program's by a relative error of at most 0.007.
Values may be sent and summed in bfloat16 or wider, within the bound.
A program may use at most 64 MiB of HBM per device.

```python
import math
import jax
import jax.numpy as jnp
import numpy as np
from jax import lax

EMB = 128
TABLES = 26
RANK = 512
HID = 1024
VOCAB = 1024
B_GRP = 1024
DIN = 3456
GROUPS = 32
TENANTS = 32
SAMPLES = 32768
CAP = 40
SLOTS = 32


def draw_table_slot(key, part):
    key = jax.random.fold_in(key, 7)
    ordering = jax.random.permutation(key, jnp.arange(SLOTS, dtype=jnp.int32))
    where_last = jnp.argmax(ordering == SLOTS - 1).astype(jnp.int32)
    leading = ordering[0]
    beyond = where_last >= TABLES
    ordering = ordering.at[where_last].set(jnp.where(beyond, leading, SLOTS - 1))
    ordering = ordering.at[0].set(jnp.where(beyond, SLOTS - 1, leading))
    return ordering[:TABLES].astype(jnp.int32)


def with_ends(drawn, own_key, least, top_value):
    shape = drawn.shape
    index_at = [jax.random.randint(jax.random.fold_in(own_key, axis), (), 0, shape[axis]) for axis in range(len(shape))]
    drawn = drawn.at[tuple(index_at)].set(least)
    longest = shape.index(max(shape))
    index_at[longest] = (index_at[longest] + 1) % shape[longest]
    return drawn.at[tuple(index_at)].set(top_value)


def block_levels(rng, dims, split, smallest, high):
    factor_of, own = 1.0, jax.random.fold_in(rng, 6)
    for axis_at, blocks in split:
        draws = jnp.exp(jax.random.uniform(jax.random.fold_in(own, axis_at), (blocks,), jnp.float32, smallest / len(split), high / len(split)))
        factor_of = factor_of * jnp.repeat(draws, dims[axis_at] // blocks).reshape([-1 if axis == axis_at else 1 for axis in range(len(dims))])
    return factor_of


def rank_table(number_of, lean):
    portions = [(1 << 20) // math.isqrt(grade ** lean) + 1 for grade in range(1, number_of + 1)]
    spread = 1 + sum(portions) // (1 << 30)
    return np.cumsum(np.array([max(1, weight // spread) for weight in portions]))


def ranked_ids(key, shape, count, slope):
    table = rank_table(count, slope)
    ticket = jax.random.randint(jax.random.fold_in(key, 1), shape, 0, int(table[count - 1]))
    standing = jnp.searchsorted(jnp.asarray(table, jnp.int32), ticket, side="right")
    return jax.random.permutation(jax.random.fold_in(key, 2), count)[standing].astype(jnp.int32)


def assign_block(stream_key, own, number, rows, number_of, top, bound, slope):
    order = jax.random.permutation(stream_key, number_of)
    packed, usual = portions_of(number_of, rows * top, bound, slope, True), portions_of(number_of, rows * top, bound, slope, False)
    places = jnp.arange(number_of)

    def named(sizes, offset_by):
        used = int((sizes > 0).sum())
        fixed = max(1, used // 4)
        moved = fixed + (places - fixed + offset_by * (used - fixed)) % max(1, number_of - fixed)
        return jnp.zeros((number_of,), jnp.int32).at[order[jnp.where(places < fixed, places, moved)]].set(jnp.asarray(sizes, jnp.int32))

    sizes = jnp.where(number % 4 == 0, named(packed, number // 4), named(usual, number - number // 4 - 1))
    mixed = jax.random.permutation(jax.random.fold_in(own, 3), number_of)
    source_of, sink = mixed[0:number_of // 2 * 2:2], mixed[1:number_of // 2 * 2:2]
    room = jnp.minimum(sizes[source_of] - 1, bound - sizes[sink]) // 2
    room = jnp.where((source_of == order[0]) | (sink == order[0]) | (sizes[sink] == 0), 0, jnp.maximum(room, 0))
    moved = jax.random.randint(jax.random.fold_in(own, 4), (number_of // 2,), 0, 1 << 20) % (room + 1)
    sizes = sizes.at[source_of].add(-moved).at[sink].add(moved)
    labels = jnp.searchsorted(jnp.cumsum(sizes), jnp.arange(rows * top), side="right").astype(jnp.int32)
    table = labels.reshape(top, rows).T
    table = table[jax.random.permutation(jax.random.fold_in(own, 1), rows)]
    offset_by = jax.random.randint(jax.random.fold_in(own, 2), (rows, 1), 0, top)
    return jnp.take_along_axis(table, (jnp.arange(top)[None, :] + offset_by) % top, axis=1)


def portions_of(number_of, total, reach, slope, full):
    loads = [(1 << 20) // math.isqrt(standing ** slope) + 1 for standing in range(1, number_of + 1)]
    largest = reach if full else min(reach, max(-(-total // number_of), total * loads[0] // sum(loads)))
    least = 1 if total - largest >= number_of - 1 else 0
    given, spare = [largest] + [least] * (number_of - 1), total - largest - least * (number_of - 1)
    while spare > 0:
        free = [i for i in range(1, number_of) if given[i] < largest] or [i for i in range(1, number_of) if given[i] < reach]
        whole, budget = sum([loads[i] for i in free]), spare
        for i in free:
            extra = min(reach - given[i], max(1, budget * loads[i] // whole), spare)
            given[i] = given[i] + extra
            spare = spare - extra
    return np.array(given)


def bell_draw(rng, dims, width, reach, shards=(), held_as=jnp.bfloat16):
    drawn = width * jax.random.normal(rng, dims, jnp.float32)
    if shards:
        drawn = drawn * block_levels(rng, dims, shards, -0.22, 0.18)
    return jnp.clip(drawn, -reach, reach).astype(held_as)


def setup_inputs(seed: int = 0) -> dict:
    keys = jax.random.split(jax.random.key(seed), 11)
    cross_in = bell_draw(keys[0], (SAMPLES, DIN), 1.0, 6.0, ((0, 32), (1, 16)))
    rank_act = bell_draw(keys[1], (SAMPLES, RANK), 1.0, 6.0, ((0, 32),))
    tower_cot = bell_draw(keys[2], (SAMPLES, HID), 1.0, 6.0, ((0, 32),))
    tenant_ids_keys = jax.random.split(jax.random.fold_in(keys[3], 1), SAMPLES // B_GRP)
    tenant_ids_turns = jax.random.permutation(jax.random.fold_in(keys[3], 3), SAMPLES // B_GRP)
    tenant_ids = jax.vmap(lambda own, number: assign_block(jax.random.fold_in(keys[3], 2), own, number, B_GRP, TENANTS, 1, CAP, 2))(tenant_ids_keys, tenant_ids_turns).reshape((SAMPLES, 1))
    sparse_ids = with_ends(ranked_ids(keys[4], (SAMPLES, TABLES), VOCAB, 2), jax.random.fold_in(keys[4], 3), 0, VOCAB - 1).astype(jnp.int32)
    table_slot = draw_table_slot(jax.random.fold_in(keys[10], 71), 0)
    cross_u = bell_draw(keys[6], (DIN, RANK), RANK ** -0.5, 0.25, ((0, 16),))
    cross_v = bell_draw(keys[7], (DIN, RANK), DIN ** -0.5, 0.109375, ((0, 16),))
    cross_bias = jnp.clip(jax.random.uniform(keys[8], (DIN,), jnp.float32, -1.0, 1.0) * block_levels(keys[8], (DIN,), ((0, 16),), -0.4, 0.0), -1.0, 1.0)
    tower_w = bell_draw(keys[9], (TENANTS, DIN, HID), HID ** -0.5, 0.1875, ((0, 32), (1, 16)))
    return dict(cross_in=cross_in, rank_act=rank_act, tower_cot=tower_cot, tenant_ids=tenant_ids, sparse_ids=sparse_ids, table_slot=table_slot, cross_u=cross_u, cross_v=cross_v, cross_bias=cross_bias, tower_w=tower_w)


def reference(cross_in, rank_act, tower_cot, tenant_ids, sparse_ids, table_slot, cross_u, cross_v, cross_bias, tower_w):
    grad_scale = 1.0 / math.sqrt(SAMPLES)
    rank_up = jnp.dot(rank_act, cross_u.T, preferred_element_type=jnp.float32)
    shifted = rank_up + cross_bias[None, :]
    inputs_wide = cross_in.astype(jnp.float32)
    crossed = (inputs_wide * shifted + inputs_wide).astype(jnp.bfloat16)
    tenant = tenant_ids[:, 0].reshape(GROUPS, B_GRP)
    member = (tenant[:, :, None] == jnp.arange(TENANTS, dtype=jnp.int32)[None, None, :]).astype(jnp.int32)
    before = jnp.cumsum(member, axis=1) - member
    position = lax.optimization_barrier(jnp.sum(before * member, axis=2))
    group_ids = jnp.arange(GROUPS, dtype=jnp.int32)[:, None]
    bucket_index = tenant * (GROUPS * CAP) + group_ids * CAP + position
    source = jnp.full((TENANTS * GROUPS * CAP,), SAMPLES, jnp.int32)
    source = source.at[bucket_index.reshape(-1)].set(jnp.arange(SAMPLES, dtype=jnp.int32))
    source = source.reshape(TENANTS, GROUPS * CAP)
    crossed_pad = jnp.concatenate([crossed, jnp.zeros((1, DIN), jnp.bfloat16)], axis=0)
    cot_pad = jnp.concatenate([tower_cot, jnp.zeros((1, HID), jnp.bfloat16)], axis=0)

    def per_tenant(tenant_item):
        weight, picked = tenant_item
        tenant_rows = jnp.take(crossed_pad, picked, axis=0)
        tenant_cot = jnp.take(cot_pad, picked, axis=0)
        grad_weight = jnp.dot(tenant_rows.T, tenant_cot, preferred_element_type=jnp.float32)
        back_rows = jnp.dot(tenant_cot, weight.T, preferred_element_type=jnp.float32)
        return ((grad_weight * grad_scale).astype(jnp.bfloat16), back_rows)
    tower_wgrad, back_parts = lax.map(per_tenant, (tower_w, source))
    back_grad = jnp.zeros((SAMPLES + 1, DIN), jnp.float32)
    back_grad = back_grad.at[source.reshape(-1)].set(back_parts.reshape(-1, DIN))[:SAMPLES]
    gate_grad = (back_grad * inputs_wide).astype(jnp.bfloat16)
    rank_grad = jnp.dot(gate_grad, cross_u, preferred_element_type=jnp.float32)
    rank_round = rank_grad.astype(jnp.bfloat16)
    input_grad = (back_grad * (shifted + 1.0) + jnp.dot(rank_round, cross_v.T, preferred_element_type=jnp.float32)).astype(jnp.bfloat16)
    cross_ugrad = jnp.dot(gate_grad.T, rank_act, preferred_element_type=jnp.float32) * grad_scale
    cross_vgrad = jnp.dot(cross_in.T, rank_round, preferred_element_type=jnp.float32) * grad_scale
    cross_bgrad = lax.optimization_barrier(jnp.sum(gate_grad.astype(jnp.float32), axis=0)) * grad_scale
    blocks = input_grad.reshape(GROUPS, B_GRP, TABLES + 1, EMB)
    id_blocks = sparse_ids.reshape(GROUPS, B_GRP, TABLES)

    def per_table(table_number):
        pooled = lax.dynamic_index_in_dim(blocks, table_number + 1, 2, keepdims=False)
        chosen = lax.dynamic_index_in_dim(id_blocks, table_number, 2, keepdims=False)
        onehot = (chosen[:, :, None] == jnp.arange(VOCAB, dtype=jnp.int32)[None, None, :]).astype(jnp.float32)
        summed = jnp.einsum('gbv,gbe->gve', onehot, pooled.astype(jnp.float32))
        return (summed * grad_scale).astype(jnp.bfloat16)
    table_parts = lax.map(per_table, jnp.arange(TABLES, dtype=jnp.int32))
    table_grad = jnp.zeros((GROUPS, SLOTS, VOCAB, EMB), jnp.bfloat16)
    table_grad = table_grad.at[:, table_slot].set(jnp.moveaxis(table_parts, 0, 1))
    return (tower_wgrad, cross_ugrad, cross_vgrad, cross_bgrad, table_grad)
```

```python
import functools
import math

import jax
import jax.numpy as jnp
from jax import lax
from jax.experimental import pallas as pl
from jax.experimental.pallas import tpu as pltpu
from jax.sharding import PartitionSpec as P

EMB = 128
VOCAB = 1024
WIDE = 256
MESH = pl.DeviceIdType.MESH
F32 = jnp.float32
BF16 = jnp.bfloat16


def mm(a, b):
    return jnp.dot(a, b, preferred_element_type=F32)


def mm_nt(a, b):
    return lax.dot_general(a, b, (((1,), (1,)), ((), ())), preferred_element_type=F32)


def mm_tn(a, b):
    return lax.dot_general(a, b, (((0,), (0,)), ((), ())), preferred_element_type=F32)


def fused(
    nd,
    nt,
    nz,
    cap,
    scale,
    inv_ref,
    ids_ref,
    xin_ref,
    rank_ref,
    cot_ref,
    u_ref,
    v_ref,
    bias_ref,
    w_ref,
    wg_out,
    u_out,
    v_out,
    b_out,
    tab_out,
    uv,
    xinp,
    crp,
    wp,
    tgt,
    perm_t,
    send,
    got,
    cotr,
    crr,
    rsend,
    rgot,
    backb,
    bh,
    gate_h,
    xgot,
    bgot,
    shift,
    rr_all,
    igp,
    igs,
    s5,
    tgot,
    hot,
    part,
    pgot,
    pred,
    pall,
    a_send,
    a_recv,
    r_send,
    r_recv,
    x_send,
    x_recv,
    b_send,
    b_recv,
    uv_send,
    uv_recv,
    sib_send,
    sib_recv,
    rr_send,
    rr_recv,
    t_send,
    t_recv,
    p_send,
    p_recv,
    q_send,
    q_recv,
):
    groups = nd * nt
    rows, width = xin_ref.shape
    rank = rank_ref.shape[1]
    half_rank = rank // 2
    hid = cot_ref.shape[1]
    half_hid = hid // 2
    chunk = rows // nz
    block = nt * cap
    uv_rows = (width + 3 + 15) // 16 * 16
    base = width // 16 * 16
    piece = WIDE // groups
    slots = tab_out.shape[0]

    dp = lax.axis_index("dp")
    tn = lax.axis_index("tenant")
    mp = lax.axis_index("mp")
    me = dp * nt + tn
    core = lax.rem(tn, 2)

    def plane(peer):
        return (peer // nt, lax.rem(peer, nt), mp)

    def column(z):
        return (dp, tn, z)

    def remote(src, dst, ssem, rsem, device):
        return pltpu.make_async_remote_copy(
            src_ref=src,
            dst_ref=dst,
            send_sem=ssem,
            recv_sem=rsem,
            device_id=device,
            device_id_type=MESH,
        )

    uv[:, :, 0, base:, :] = jnp.zeros((nz, 2, WIDE - base, half_rank), BF16)

    barrier = pltpu.get_barrier_semaphore()

    def greet_plane(o, carry):
        pl.semaphore_signal(barrier, inc=1, device_id=plane(lax.rem(me + o, groups)), device_id_type=MESH)
        return carry

    def greet_column(o, carry):
        pl.semaphore_signal(barrier, inc=1, device_id=column(lax.rem(mp + o, nz)), device_id_type=MESH)
        return carry

    lax.fori_loop(1, groups, greet_plane, 0)
    lax.fori_loop(1, nz, greet_column, 0)

    bias = jnp.concatenate([bias_ref[...], jnp.zeros((1, WIDE - width), F32)], axis=1)
    hi = bias.astype(BF16).astype(F32)
    mid = (bias - hi).astype(BF16).astype(F32)
    low = bias - hi - mid
    bias_rows = [hi, mid, low, jnp.zeros((uv_rows - width - 3, WIDE), F32)]
    for h in range(2):
        cols = slice(h * half_rank, (h + 1) * half_rank)
        uv[mp, h, 0, 0:base] = u_ref[0:base, cols]
        tail = bias_rows
        if base < width:
            tail = [u_ref[base:width, cols].astype(F32)] + bias_rows
        uv[mp, h, 0, base:uv_rows] = jnp.concatenate(tail, axis=0).astype(BF16)
        uv[mp, h, 1, 0:width] = v_ref[:, cols]
    xinp[:, 0:128] = xin_ref[:, 0:128]
    xinp[:, 128:WIDE] = jnp.concatenate(
        [xin_ref[:, 128:width].astype(F32), jnp.zeros((rows, WIDE - width), F32)], axis=1
    ).astype(BF16)
    whole = (width - 1) // 16 * 16
    wp[0:whole] = w_ref[0:whole]
    wp[whole:WIDE] = jnp.concatenate(
        [w_ref[whole:width].astype(F32), jnp.zeros((WIDE - width, hid), F32)], axis=0
    ).astype(BF16)

    tenant = ids_ref[0:1, :]
    member = lax.broadcasted_iota(jnp.int32, (groups, rows), 0) == tenant
    earlier = lax.broadcasted_iota(jnp.int32, (rows, rows), 0) < lax.broadcasted_iota(
        jnp.int32, (rows, rows), 1
    )
    before = mm(member.astype(F32).astype(BF16), earlier.astype(F32).astype(BF16))
    position = jnp.sum(jnp.where(member, before, 0.0), axis=0, keepdims=True)
    target = tenant * cap + position.astype(jnp.int32)
    tgt[...] = jnp.broadcast_to(target, tgt.shape)

    pl.semaphore_wait(barrier, groups - 1 + nz - 1)

    right, left = lax.rem(mp + 1, nz), lax.rem(mp + nz - 1, nz)
    sibling = (dp, tn + 1 - 2 * core, mp)
    half_ring = nz // 2

    def uv_copy(c, way, step):
        spot = uv.at[c, core, :, 0:uv_rows]
        return remote(spot, spot, uv_send.at[way, step], uv_recv.at[c], column(right if way == 0 else left))

    def sib_copy(c):
        spot = uv.at[c, core, :, 0:uv_rows]
        return remote(spot, spot, sib_send.at[c], sib_recv.at[c], sibling)

    def uv_ring(step):
        came = lax.rem(mp + nz - step, nz)
        uv_copy(came, 0, step - 1).wait_recv()

        @pl.when(step < half_ring)
        def _():
            uv_copy(came, 0, step).start()

        sib_copy(came).start()

        @pl.when(step < half_ring)
        def _():
            other = lax.rem(mp + step, nz)
            uv_copy(other, 1, step - 1).wait_recv()

            @pl.when(step < half_ring - 1)
            def _():
                uv_copy(other, 1, step).start()

            sib_copy(other).start()

    uv_copy(mp, 0, 0).start()
    uv_copy(mp, 1, 0).start()

    rank_up = mm_nt(rank_ref[:, 0:half_rank], uv[mp, 0, 0]) + mm_nt(
        rank_ref[:, half_rank:rank], uv[mp, 1, 0]
    )
    wide = xinp[...].astype(F32)
    crp[...] = (wide * (rank_up + bias) + wide).astype(BF16)

    def a_copy(peer, source):
        return remote(send.at[peer], got.at[source], a_send.at[peer], a_recv.at[source], plane(peer))

    def bucket(k, carry):
        to = lax.rem(dp + k, nd)
        chosen = lax.broadcasted_iota(jnp.int32, (block, rows), 0) + to * block == tgt[0:1, :]
        chosen = chosen.astype(F32).astype(BF16)
        cots = mm(chosen, cot_ref[...])
        crossed = mm(chosen, crp[...])
        for j in range(nt):
            s = slice(j * cap, (j + 1) * cap)
            send[to * nt + j] = jnp.concatenate(
                [
                    jnp.concatenate([cots[s, 0:half_hid], crossed[s, 0:128]], axis=1),
                    jnp.concatenate([cots[s, half_hid:hid], crossed[s, 128:WIDE]], axis=1),
                ],
                axis=0,
            ).astype(BF16)

        def start(o, inner):
            peer = to * nt + lax.rem(tn + o, nt)

            @pl.when(peer != me)
            def _():
                a_copy(peer, me).start()

            return inner

        lax.fori_loop(0, nt, start, 0)
        return carry

    lax.fori_loop(0, nd, bucket, 0)
    got[me] = send[me]

    target_col = jnp.transpose(tgt[...].astype(F32))[:, 0:1].astype(jnp.int32)
    perm_t[...] = (
        (lax.broadcasted_iota(jnp.int32, perm_t.shape, 1) == target_col).astype(F32).astype(BF16)
    )

    uv_ring(1)

    def x_copy(z, source):
        return remote(
            xinp.at[pl.ds(pl.multiple_of(z * chunk, chunk), chunk)],
            xgot.at[source],
            x_send.at[z],
            x_recv.at[source],
            column(z),
        )

    def each_z(body):
        def run(o, carry):
            body(lax.rem(mp + o, nz))
            return carry

        lax.fori_loop(1, nz, run, 0)

    def each_peer(body):
        def run(o, carry):
            body(lax.rem(me + o, groups))
            return carry

        lax.fori_loop(1, groups, run, 0)

    each_z(lambda z: x_copy(z, mp).start())
    xgot[mp] = xinp[pl.ds(pl.multiple_of(mp * chunk, chunk), chunk)]

    def r_copy(peer, source):
        return remote(rsend.at[peer], rgot.at[source], r_send.at[peer], r_recv.at[source], plane(peer))

    def owner(k, carry):
        frm = lax.rem(dp + nd - k, nd)

        @pl.when(k + 2 <= half_ring)
        def _():
            uv_ring(k + 2)

        def arrive(o, inner):
            peer = frm * nt + o

            @pl.when(peer != me)
            def _():
                a_copy(me, peer).wait_recv()

            return inner

        lax.fori_loop(0, nt, arrive, 0)
        cots, crossed = [], []
        for j in range(nt):
            blk = got[frm * nt + j].astype(F32)
            cots.append(jnp.concatenate([blk[0:cap, 0:half_hid], blk[cap:, 0:half_hid]], axis=1))
            crossed.append(jnp.concatenate([blk[0:cap, half_hid:], blk[cap:, half_hid:]], axis=1))
        cots = jnp.concatenate(cots, axis=0).astype(BF16)
        at = pl.ds(pl.multiple_of(frm * block, block), block)
        cotr[at] = cots
        crr[at] = jnp.concatenate(crossed, axis=0).astype(BF16)
        back = mm_nt(cots, wp[...])
        for j in range(nt):
            s = slice(j * cap, (j + 1) * cap)
            rsend[frm * nt + j] = jnp.concatenate(
                [back[s, 0:128], back[s, 128:WIDE]], axis=0
            ).astype(BF16)

        def start(o, inner):
            peer = frm * nt + lax.rem(tn + o, nt)

            @pl.when(peer != me)
            def _():
                r_copy(peer, me).start()

            return inner

        lax.fori_loop(0, nt, start, 0)
        return carry

    lax.fori_loop(0, nd, owner, 0)
    rgot[me] = rsend[me]

    wgrad = mm_tn(crr[...], cotr[...])
    wg_out[...] = (wgrad[0:width] * scale).astype(BF16)

    each_peer(lambda p: r_copy(me, p).wait_recv())

    def unpack(t, carry):
        pair = []
        for j in range(2):
            blk = rgot[2 * t + j].astype(F32)
            pair.append(jnp.concatenate([blk[0:cap], blk[cap:]], axis=1))
        backb[pl.ds(pl.multiple_of(t * 2 * cap, 2 * cap), 2 * cap)] = jnp.concatenate(
            pair, axis=0
        ).astype(BF16)
        return carry

    lax.fori_loop(0, groups // 2, unpack, 0)
    bh[...] = mm(perm_t[...], backb[...]).astype(BF16)

    def b_copy(z, source):
        return remote(
            bh.at[pl.ds(pl.multiple_of(z * chunk, chunk), chunk)],
            bgot.at[source],
            b_send.at[z],
            b_recv.at[source],
            column(z),
        )

    each_z(lambda z: b_copy(z, mp).start())
    bgot[mp] = bh[pl.ds(pl.multiple_of(mp * chunk, chunk), chunk)]

    def p_copy(i, peer, source):
        return remote(
            part.at[i, pl.ds(pl.multiple_of(peer * piece, piece), piece)],
            pgot.at[i, source],
            p_send.at[i, peer],
            p_recv.at[i, source],
            plane(peer),
        )

    def q_copy(i, peer, source):
        return remote(
            pred.at[i],
            pall.at[i, pl.ds(pl.multiple_of(source * piece, piece), piece)],
            q_send.at[i, peer],
            q_recv.at[i, source],
            plane(peer),
        )

    def scatter(i):
        each_peer(lambda p: p_copy(i, p, me).start())
        pgot[i, me] = part[i, pl.ds(pl.multiple_of(me * piece, piece), piece)]

    def gather(i):
        each_peer(lambda p: p_copy(i, me, p).wait_recv())
        total = jnp.sum(pgot[i], axis=0) * scale
        pred[i] = total
        pall[i, pl.ds(pl.multiple_of(me * piece, piece), piece)] = total
        each_peer(lambda p: q_copy(i, p, me).start())

    gate_h[...] = (bh[...].astype(F32) * xinp[...].astype(F32)).astype(BF16)
    part[0] = mm_tn(gate_h[...], rank_ref[...])
    part[0, width : width + 8, 0:WIDE] = mm(jnp.ones((8, rows), BF16), gate_h[...])
    scatter(0)

    for step in range(nd + 2, half_ring + 1):
        uv_ring(step)
    each_z(lambda z: sib_copy(z).wait_recv())

    rank_here = rank_ref[pl.ds(pl.multiple_of(mp * chunk, chunk), chunk), :]

    def shift_of(z, carry):
        ends = uv[z, 0, 0, base:uv_rows].astype(F32)
        first = width - base
        bias_z = ends[first : first + 1] + ends[first + 1 : first + 2] + ends[first + 2 : first + 3]
        up = mm_nt(rank_here[:, 0:half_rank], uv[z, 0, 0]) + mm_nt(
            rank_here[:, half_rank:rank], uv[z, 1, 0]
        )
        shift[z] = up + bias_z + 1.0
        return carry

    lax.fori_loop(0, nz, shift_of, 0)

    for k in range(slots):
        table = inv_ref[mp * slots + k]
        ids = jnp.sum(
            jnp.where(lax.broadcasted_iota(jnp.int32, ids_ref.shape, 0) == table, ids_ref[...], 0),
            axis=0,
            keepdims=True,
        )
        hot[k] = (lax.broadcasted_iota(jnp.int32, (VOCAB, rows), 0) == ids).astype(F32).astype(BF16)

    gather(0)

    each_z(lambda z: x_copy(mp, z).wait_recv())
    each_z(lambda z: b_copy(mp, z).wait_recv())

    def rank_of(z, total):
        gate = (bgot[z].astype(F32) * xgot[z].astype(F32)).astype(BF16)
        return total[0] + mm(gate, uv[z, 0, 0]), total[1] + mm(gate, uv[z, 1, 0])

    zero = jnp.zeros((chunk, half_rank), F32)
    lo, up = lax.fori_loop(0, nz, rank_of, (zero, zero))
    rr = jnp.concatenate([lo, up], axis=1).astype(BF16)
    rr_all[mp] = rr

    def rr_copy(c, way, step):
        return remote(
            rr_all.at[c],
            rr_all.at[c],
            rr_send.at[way, step],
            rr_recv.at[c],
            column(right if way == 0 else left),
        )

    rr_copy(mp, 0, 0).start()
    rr_copy(mp, 1, 0).start()

    def input_of(z, carry):
        igp[z] = bgot[z].astype(F32) * shift[z] + (
            mm_nt(rr[:, 0:half_rank], uv[z, 0, 1]) + mm_nt(rr[:, half_rank:rank], uv[z, 1, 1])
        )
        return carry

    lax.fori_loop(0, nz, input_of, 0)
    igs[0] = jnp.zeros((chunk, EMB), BF16)
    for t in range(1, igs.shape[0]):
        pieces, at = [], t * EMB
        while at < (t + 1) * EMB:
            z, first = at // width, at % width
            stop = min(width, first + (t + 1) * EMB - at)
            pieces.append(igp[z][:, first:stop])
            at += stop - first
        igs[t] = jnp.concatenate(pieces, axis=1).astype(BF16)

    def t_copy(z, source):
        return remote(s5.at[z], tgot.at[source], t_send.at[z], t_recv.at[source], column(z))

    def fill(z, carry):
        for k in range(slots):
            s5[z, k] = igs[inv_ref[z * slots + k]]
        return carry

    lax.fori_loop(0, nz, fill, 0)
    each_z(lambda z: t_copy(z, mp).start())
    tgot[mp] = s5[mp]

    def rr_ring(step, carry):
        came = lax.rem(mp + nz - step, nz)
        rr_copy(came, 0, step - 1).wait_recv()

        @pl.when(step < half_ring)
        def _():
            rr_copy(came, 0, step).start()
            other = lax.rem(mp + step, nz)
            rr_copy(other, 1, step - 1).wait_recv()

            @pl.when(step < half_ring - 1)
            def _():
                rr_copy(other, 1, step).start()

        return carry

    lax.fori_loop(1, half_ring + 1, rr_ring, 0)

    part[1] = mm_tn(xinp[...], rr_all[...].reshape(rows, rank))
    scatter(1)

    each_z(lambda z: t_copy(mp, z).wait_recv())
    for k in range(slots):
        values = tgot[:, k].reshape(rows, EMB)
        tab_out[k] = (mm(hot[k], values) * scale).astype(BF16)

    gather(1)
    for i, out in ((0, u_out), (1, v_out)):
        each_peer(lambda p: q_copy(i, me, p).wait_recv())
        out[...] = pall[i, 0:width]
    b_out[...] = pall[0, width : width + 1, 0:width]

    def left_plane(p):
        a_copy(p, me).wait_send()
        r_copy(p, me).wait_send()
        for i in range(2):
            p_copy(i, p, me).wait_send()
            q_copy(i, p, me).wait_send()

    def left_column(z):
        x_copy(z, mp).wait_send()
        b_copy(z, mp).wait_send()
        t_copy(z, mp).wait_send()
        sib_copy(z).wait_send()

    each_peer(left_plane)
    each_z(left_column)
    for step in range(half_ring):
        uv_copy(mp, 0, step).wait_send()
        rr_copy(mp, 0, step).wait_send()
        if step < half_ring - 1:
            uv_copy(mp, 1, step).wait_send()
            rr_copy(mp, 1, step).wait_send()


def on_device(
    cross_in,
    rank_act,
    tower_cot,
    tenant_ids,
    sparse_ids,
    table_slot,
    cross_u,
    cross_v,
    cross_bias,
    tower_w,
):
    nd, nt, nz = lax.axis_size("dp"), lax.axis_size("tenant"), lax.axis_size("mp")
    groups = nd * nt
    rows, width = cross_in.shape
    rank, hid = rank_act.shape[1], tower_cot.shape[1]
    tables = table_slot.shape[0]
    slots = (tables + nz - 1) // nz
    cap = (5 * rows + 4 * groups - 1) // (4 * groups)
    chunk = rows // nz
    half_ring = nz // 2
    scale = 1.0 / math.sqrt(rows * groups)

    taken = table_slot[:, None] == jnp.arange(nz * slots, dtype=jnp.int32)[None, :]
    numbers = jnp.arange(1, tables + 1, dtype=jnp.int32)[:, None]
    inverse = jnp.sum(jnp.where(taken, numbers, 0), axis=0)
    ids = jnp.concatenate([tenant_ids, sparse_ids], axis=1).T

    vmem = pl.BlockSpec(memory_space=pltpu.VMEM)
    smem = pl.BlockSpec(memory_space=pltpu.SMEM)
    sem = pltpu.SemaphoreType.DMA

    def bf(*shape):
        return pltpu.VMEM(shape, BF16)

    def ff(*shape):
        return pltpu.VMEM(shape, F32)

    out = pl.pallas_call(
        functools.partial(fused, nd, nt, nz, cap, scale),
        out_shape=(
            jax.ShapeDtypeStruct((width, hid), BF16),
            jax.ShapeDtypeStruct((width, rank), F32),
            jax.ShapeDtypeStruct((width, rank), F32),
            jax.ShapeDtypeStruct((1, width), F32),
            jax.ShapeDtypeStruct((slots, VOCAB, EMB), BF16),
        ),
        in_specs=[smem] + [vmem] * 8,
        out_specs=(vmem,) * 5,
        scratch_shapes=[
            bf(nz, 2, 2, WIDE, rank // 2),
            bf(rows, WIDE),
            bf(rows, WIDE),
            bf(WIDE, hid),
            pltpu.VMEM((8, rows), jnp.int32),
            bf(rows, groups * cap),
            bf(groups, 2 * cap, hid // 2 + 128),
            bf(groups, 2 * cap, hid // 2 + 128),
            bf(groups * cap, hid),
            bf(groups * cap, WIDE),
            bf(groups, 2 * cap, 128),
            bf(groups, 2 * cap, 128),
            bf(groups * cap, WIDE),
            bf(rows, WIDE),
            bf(rows, WIDE),
            bf(nz, chunk, WIDE),
            bf(nz, chunk, WIDE),
            ff(nz, chunk, WIDE),
            bf(nz, chunk, rank),
            ff(nz, chunk, WIDE),
            bf(tables + 1, chunk, EMB),
            bf(nz, slots, chunk, EMB),
            bf(nz, slots, chunk, EMB),
            bf(slots, VOCAB, rows),
            ff(2, WIDE, rank),
            ff(2, groups, WIDE // groups, rank),
            ff(2, WIDE // groups, rank),
            ff(2, WIDE, rank),
            sem((groups,)),
            sem((groups,)),
            sem((groups,)),
            sem((groups,)),
            sem((nz,)),
            sem((nz,)),
            sem((nz,)),
            sem((nz,)),
            sem((2, half_ring)),
            sem((nz,)),
            sem((nz,)),
            sem((nz,)),
            sem((2, half_ring)),
            sem((nz,)),
            sem((nz,)),
            sem((nz,)),
            sem((2, groups)),
            sem((2, groups)),
            sem((2, groups)),
            sem((2, groups)),
        ],
        compiler_params=pltpu.CompilerParams(
            collective_id=0, has_side_effects=True, vmem_limit_bytes=60 * 2**20
        ),
    )(
        inverse,
        ids,
        cross_in,
        rank_act,
        tower_cot,
        cross_u,
        cross_v,
        cross_bias[None, :],
        tower_w[0],
    )
    wgrad, u_total, v_total, b_total, table = out
    return wgrad[None], u_total, v_total, b_total[0], table[None]


def solution(mesh):
    return jax.shard_map(
        on_device,
        mesh=mesh,
        in_specs=(
            P(("dp", "tenant"), "mp"),
            P(("dp", "tenant"), None),
            P(("dp", "tenant"), None),
            P(("dp", "tenant"), None),
            P(("dp", "tenant"), None),
            P(),
            P("mp", None),
            P("mp", None),
            P("mp"),
            P(("dp", "tenant"), "mp", None),
        ),
        out_specs=(
            P(("dp", "tenant"), "mp", None),
            P("mp", None),
            P("mp", None),
            P("mp"),
            P(("dp", "tenant"), "mp", None, None),
        ),
        check_vma=False,
    )
```

```python
import functools
import math

import jax
import jax.numpy as jnp
from jax import lax
from jax.experimental import pallas as pl
from jax.experimental.pallas import tpu as pltpu
from jax.sharding import PartitionSpec as P

EMB = 128
VOCAB = 1024
T_SENT = (2, 4, 6, 8, 12)
WIDE = 256
MESH = pl.DeviceIdType.MESH
F32 = jnp.float32
BF16 = jnp.bfloat16


def mm(a, b):
    return jnp.dot(a, b, preferred_element_type=F32)


def mm_nt(a, b):
    return lax.dot_general(a, b, (((1,), (1,)), ((), ())), preferred_element_type=F32)


def mm_tn(a, b):
    return lax.dot_general(a, b, (((0,), (0,)), ((), ())), preferred_element_type=F32)


def fused(
    nd,
    nt,
    nz,
    cap,
    scale,
    slot_ref,
    tenant_hbm,
    xin_hbm,
    u_hbm,
    rank_hbm,
    bias_hbm,
    cot_hbm,
    v_hbm,
    w_hbm,
    ids_hbm,
    wg_hbm,
    u_out_hbm,
    v_out_hbm,
    b_out_hbm,
    tab_hbm,
    tenant_ref,
    xin_ref,
    u_ref,
    rank_ref,
    bias_ref,
    cot_ref,
    v_ref,
    w_ref,
    ids_ref,
    wg_out,
    tab_out,
    inv_ref,
    in_sem,
    out_sem,
    uo,
    bo,
    uv,
    up,
    vp,
    xin_t,
    xinp,
    crp,
    wp,
    tgt,
    perm_t,
    send,
    got,
    cotr,
    crr,
    rsend,
    rgot,
    backb,
    bh,
    gate_h,
    xgot,
    bgot,
    shift,
    rr_all,
    igp,
    igs,
    s5,
    tgot,
    hot,
    part,
    pgot,
    pred,
    pall,
    tally,
    a_send,
    a_recv,
    r_sem,
    x_sem,
    b_sem,
    uv_send,
    uv_recv,
    sib_send,
    sib_recv,
    swap_send,
    swap_recv,
    late_send,
    late_recv,
    rr_send,
    rr_recv,
    t_sem,
    p_sem,
    q_sem,
):
    groups = nd * nt
    width, rows = xin_ref.shape
    rank = rank_ref.shape[1]
    half_rank = rank // 2
    hid = cot_ref.shape[1]
    half_hid = hid // 2
    chunk = rows // nz
    block = nt * cap
    uv_rows = (width + 3 + 15) // 16 * 16
    base = width // 16 * 16
    piece = 2 * WIDE // groups
    per_half = groups // 2
    slots = tab_out.shape[0]

    dp = lax.axis_index("dp")
    tn = lax.axis_index("tenant")
    mp = lax.axis_index("mp")
    me = dp * nt + tn
    core = lax.rem(tn, 2)
    across = tn // 2
    nx = nt // 2

    def partner(o):
        k, a, c = o // (2 * nd), lax.rem(nd - lax.rem(o // 2, nd), nd), lax.rem(o, 2)
        there = lax.rem(across + a + k, nx)
        return lax.rem(dp + a, nd) * nt + 2 * there + lax.rem(core + c, 2)

    def plane(peer):
        return (peer // nt, lax.rem(peer, nt), mp)

    def column(z):
        return (dp, tn, z)

    def remote(src, dst, ssem, rsem, device):
        return pltpu.make_async_remote_copy(
            src_ref=src,
            dst_ref=dst,
            send_sem=ssem,
            recv_sem=rsem,
            device_id=device,
            device_id_type=MESH,
        )

    pairs = [
        (tenant_hbm, tenant_ref),
        (xin_hbm, xin_ref),
        (u_hbm, u_ref),
        (rank_hbm, rank_ref),
        (bias_hbm, bias_ref),
        (cot_hbm, cot_ref),
        (v_hbm, v_ref),
        (w_hbm, w_ref),
        (ids_hbm, ids_ref),
    ]
    loads = [pltpu.make_async_copy(a, b, in_sem.at[i]) for i, (a, b) in enumerate(pairs)]
    for load in loads:
        load.start()

    uv[:, :, 0, uv_rows:, :] = jnp.zeros((nz, 2, WIDE - uv_rows, half_rank), BF16)

    barrier = pltpu.get_barrier_semaphore()

    def greet_plane(o, carry):
        pl.semaphore_signal(barrier, inc=1, device_id=plane(lax.rem(me + o, groups)), device_id_type=MESH)
        return carry

    def greet_column(o, carry):
        pl.semaphore_signal(barrier, inc=1, device_id=column(lax.rem(mp + o, nz)), device_id_type=MESH)
        return carry

    lax.fori_loop(1, groups, greet_plane, 0)
    lax.fori_loop(1, nz, greet_column, 0)

    for load in loads[:5]:
        load.wait()

    bias = jnp.concatenate([bias_ref[...], jnp.zeros((1, WIDE - width), F32)], axis=1)
    hi = bias.astype(BF16).astype(F32)
    mid = (bias - hi).astype(BF16).astype(F32)
    low = bias - hi - mid
    bias_rows = [hi, mid, low, jnp.zeros((WIDE - width - 3, WIDE), F32)]
    for h in range(2):
        cols = slice(h * half_rank, (h + 1) * half_rank)
        up[h, 0:base] = u_ref[0:base, cols]
        tail = bias_rows
        if base < width:
            tail = [u_ref[base:width, cols].astype(F32)] + bias_rows
        up[h, base:WIDE] = jnp.concatenate(tail, axis=0).astype(BF16)
    whole = (width - 1) // 16 * 16

    def padded(ref):
        ends = ref[whole:width].astype(F32)
        ends = jnp.concatenate([ends, jnp.zeros((WIDE - width, ref.shape[1]), F32)], axis=0)
        return ends.astype(BF16)

    xin_t[0:whole] = xin_ref[0:whole]
    xin_t[whole:WIDE] = padded(xin_ref)
    xinp[...] = jnp.transpose(xin_t[...])

    tenant = tenant_ref[...]
    member = lax.broadcasted_iota(jnp.int32, (groups, rows), 0) == tenant
    earlier = lax.broadcasted_iota(jnp.int32, (rows, rows), 0) < lax.broadcasted_iota(
        jnp.int32, (rows, rows), 1
    )
    before = mm(member.astype(F32).astype(BF16), earlier.astype(F32).astype(BF16))
    position = jnp.sum(jnp.where(member, before, 0.0), axis=0, keepdims=True)
    target = tenant * cap + position.astype(jnp.int32)
    tgt[...] = jnp.broadcast_to(target, tgt.shape)

    pl.semaphore_wait(barrier, groups - 1 + nz - 1)

    right, left = lax.rem(mp + 1, nz), lax.rem(mp + nz - 1, nz)
    sibling = (dp, tn + 1 - 2 * core, mp)
    beside = (dp, lax.rem(across + 1, 2) * 2 + across // 2 * 4 + core, mp)
    above = (dp // 2 * 2 + 1 - lax.rem(dp, 2), tn, mp)
    half_ring = nz // 2

    half_rows = uv_rows // 2
    even = lax.rem(across + dp, 2)
    mine = pl.ds(pl.multiple_of(even * half_rows, half_rows), half_rows)
    others = pl.ds(pl.multiple_of((1 - even) * half_rows, half_rows), half_rows)

    class Both:
        def __init__(self, copies):
            self.copies = copies

        def start(self):
            for copy in self.copies:
                copy.start()

        def wait_recv(self):
            for copy in self.copies:
                copy.wait_recv()

        def wait_send(self):
            for copy in self.copies:
                copy.wait_send()

    def parts(c):
        return uv.at[c, core, 0, 0:uv_rows], uv.at[c, core, 1, mine]

    def uv_copy(c, way, step):
        to = column(right if way == 0 else left)
        return Both(
            [remote(x, x, uv_send.at[i, way, step], uv_recv.at[i, c], to) for i, x in enumerate(parts(c))]
        )

    def sib_copy(c):
        return Both(
            [remote(x, x, sib_send.at[i, c], sib_recv.at[i, c], sibling) for i, x in enumerate(parts(c))]
        )

    def swap_copy(i):
        spot = uv.at[i * half_ring : (i + 1) * half_ring, core, 1, mine]
        return remote(spot, spot, swap_send.at[i], swap_recv.at[i], above if i else beside)

    def late_copy(i):
        spot = uv.at[i * half_ring : (i + 1) * half_ring, core, 1, others]
        return remote(spot, spot, late_send.at[i], late_recv.at[i], sibling)

    def uv_ring(step):
        came = lax.rem(mp + nz - step, nz)
        uv_copy(came, 0, step - 1).wait_recv()

        @pl.when(step < half_ring)
        def _():
            uv_copy(came, 0, step).start()

        sib_copy(came).start()

        @pl.when(step < half_ring)
        def _():
            other = lax.rem(mp + step, nz)
            uv_copy(other, 1, step - 1).wait_recv()

            @pl.when(step < half_ring - 1)
            def _():
                uv_copy(other, 1, step).start()

            sib_copy(other).start()

    loads[6].wait()
    for h in range(2):
        vp[h, 0:whole] = v_ref[0:whole, h * half_rank : (h + 1) * half_rank]
        vp[h, whole:WIDE] = padded(v_ref)[:, h * half_rank : (h + 1) * half_rank]
    uv[mp, core, 0, 0:uv_rows] = up[core, 0:uv_rows]
    uv[mp, core, 1, mine] = vp[core, mine]
    uv_copy(mp, 0, 0).start()
    uv_copy(mp, 1, 0).start()
    sib_copy(mp).start()

    rank_up = mm_nt(rank_ref[:, 0:half_rank], up[0]) + mm_nt(rank_ref[:, half_rank:rank], up[1])
    wide = xinp[...].astype(F32)
    crp[...] = (wide * (rank_up + bias) + wide).astype(BF16)

    loads[5].wait()

    def drain(ref, count, sem):
        spot = ref.at[pl.ds(0, count)]
        pltpu.make_async_copy(spot, spot, sem).wait()

    def a_copy(peer, k):
        return remote(send.at[peer], got.at[me], a_send.at[0], a_recv.at[k], plane(peer))

    def tenants_of(k, way):
        first = []
        for a in range(nd):
            up = lax.rem(dp + nd + way * a, nd)
            there = lax.rem(across + 2 * nx + way * lax.rem(a + k, nx), nx)
            first.append(up * nt + 2 * there)
        return first

    def bucket(k, carry):
        firsts = tenants_of(k, 1)
        spots = lax.broadcasted_iota(jnp.int32, (2 * cap, rows), 0)
        chosen = jnp.concatenate([spots + first * cap for first in firsts], axis=0) == tgt[0:1, :]
        chosen = chosen.astype(F32).astype(BF16)
        cots = mm(chosen, cot_ref[...])
        crossed = mm(chosen, crp[...])
        for j in range(2 * nd):
            s = slice(j * cap, (j + 1) * cap)
            send[firsts[j // 2] + j % 2] = jnp.concatenate(
                [
                    jnp.concatenate([cots[s, 0:half_hid], crossed[s, 0:128]], axis=1),
                    jnp.concatenate([cots[s, half_hid:hid], crossed[s, 128:WIDE]], axis=1),
                ],
                axis=0,
            ).astype(BF16)

        def start(o, inner):
            peer = partner(k * 2 * nd + o)

            @pl.when(peer != me)
            def _():
                a_copy(peer, k).start()

            return inner

        lax.fori_loop(0, 2 * nd, start, 0)
        return carry

    lax.fori_loop(0, nx, bucket, 0)
    got[me] = send[me]

    target_col = jnp.transpose(tgt[...].astype(F32))[:, 0:1].astype(jnp.int32)
    perm_t[...] = (
        (lax.broadcasted_iota(jnp.int32, perm_t.shape, 1) == target_col).astype(F32).astype(BF16)
    )

    uv_ring(1)
    loads[7].wait()
    wp[0:whole] = w_ref[0:whole]
    wp[whole:WIDE] = padded(w_ref)
    uv_ring(2)

    tables = slot_ref.shape[0]

    def invert(slot, carry):
        number = jnp.int32(0)
        for t in range(tables):
            number = jnp.where(slot_ref[t] == slot, t + 1, number)
        inv_ref[slot] = number
        return carry

    lax.fori_loop(0, nz * slots, invert, 0)
    loads[8].wait()
    for k in range(slots):
        table = inv_ref[mp * slots + k] - 1
        ids = jnp.sum(
            jnp.where(lax.broadcasted_iota(jnp.int32, ids_ref.shape, 0) == table, ids_ref[...], 0),
            axis=0,
            keepdims=True,
        )
        hot[k] = (lax.broadcasted_iota(jnp.int32, (VOCAB, rows), 0) == ids).astype(F32).astype(BF16)

    uv_ring(3)

    def x_copy(z):
        here = pl.ds(pl.multiple_of(z * chunk, chunk), chunk)
        return remote(xinp.at[here], xgot.at[mp], x_sem.at[0], x_sem.at[1], column(z))

    def each_z(body):
        def run(o, carry):
            step = (o + 1) // 2
            body(lax.rem(mp + jnp.where(lax.rem(o, 2) == 1, step, nz - step), nz))
            return carry

        lax.fori_loop(1, nz, run, 0)

    def each_peer(body):
        def run(o, carry):
            body(partner(o))
            return carry

        lax.fori_loop(1, groups, run, 0)

    xgot[mp] = xinp[pl.ds(pl.multiple_of(mp * chunk, chunk), chunk)]

    def r_copy(peer):
        return remote(rsend.at[peer], rgot.at[me], r_sem.at[0], r_sem.at[1], plane(peer))

    for step in range(4, half_ring + 1):
        uv_ring(step)
    for i in range(2):
        swap_copy(i).start()

    each_z(lambda z: x_copy(z).start())

    def owner(k, carry):
        firsts = tenants_of(k, -1)

        @pl.when(k == 0)
        def _():
            drain(got, 2 * nd - 1, a_recv.at[0])

        @pl.when(k > 0)
        def _():
            drain(got, 2 * nd, a_recv.at[k])

        cots, crossed = [], []
        for first in firsts:
            for j in range(2):
                blk = got[first + j].astype(F32)
                cots.append(jnp.concatenate([blk[0:cap, 0:half_hid], blk[cap:, 0:half_hid]], axis=1))
                crossed.append(jnp.concatenate([blk[0:cap, half_hid:], blk[cap:, half_hid:]], axis=1))
        cots = jnp.concatenate(cots, axis=0).astype(BF16)
        at = pl.ds(pl.multiple_of(k * 2 * nd * cap, 2 * nd * cap), 2 * nd * cap)
        cotr[at] = cots
        crr[at] = jnp.concatenate(crossed, axis=0).astype(BF16)
        back = mm_nt(cots, wp[...])
        for j in range(2 * nd):
            s = slice(j * cap, (j + 1) * cap)
            rsend[firsts[j // 2] + j % 2] = jnp.concatenate(
                [back[s, 0:128], back[s, 128:WIDE]], axis=0
            ).astype(BF16)
        for first in firsts:
            for j in range(2):

                @pl.when(first + j != me)
                def _():
                    r_copy(first + j).start()

        return carry

    lax.fori_loop(0, nx, owner, 0)
    rgot[me] = rsend[me]

    wgrad = mm_tn(crr[...], cotr[...])
    wg_out[...] = (wgrad[0:width] * scale).astype(BF16)
    stores = [
        pltpu.make_async_copy(wg_out, wg_hbm, out_sem.at[0]),
        pltpu.make_async_copy(uo.at[0], u_out_hbm, out_sem.at[1]),
        pltpu.make_async_copy(uo.at[1], v_out_hbm, out_sem.at[2]),
        pltpu.make_async_copy(bo, b_out_hbm, out_sem.at[3]),
        pltpu.make_async_copy(tab_out, tab_hbm, out_sem.at[4]),
    ]
    stores[0].start()

    drain(rgot, groups - 1, r_sem.at[1])

    def unpack(t, carry):
        pair = []
        for j in range(2):
            blk = rgot[2 * t + j].astype(F32)
            pair.append(jnp.concatenate([blk[0:cap], blk[cap:]], axis=1))
        backb[pl.ds(pl.multiple_of(t * 2 * cap, 2 * cap), 2 * cap)] = jnp.concatenate(
            pair, axis=0
        ).astype(BF16)
        return carry

    lax.fori_loop(0, groups // 2, unpack, 0)
    bh[...] = mm(perm_t[...], backb[...]).astype(BF16)

    def b_copy(z):
        here = pl.ds(pl.multiple_of(z * chunk, chunk), chunk)
        return remote(bh.at[here], bgot.at[mp], b_sem.at[0], b_sem.at[1], column(z))

    each_z(lambda z: b_copy(z).start())
    bgot[mp] = bh[pl.ds(pl.multiple_of(mp * chunk, chunk), chunk)]

    def piece_of(peer):
        return peer // per_half, pl.ds(pl.multiple_of(lax.rem(peer, per_half) * piece, piece), piece)

    def p_copy(i, peer):
        h, at = piece_of(peer)
        return remote(part.at[i, h, at], pgot.at[i, me], p_sem.at[i, 0], p_sem.at[i, 1], plane(peer))

    def q_copy(i, peer):
        h, at = piece_of(me)
        return remote(pred.at[i], pall.at[i, h, at], q_sem.at[i, 0], q_sem.at[i, 1], plane(peer))

    def scatter(i):
        each_peer(lambda p: p_copy(i, p).start())
        h, at = piece_of(me)
        pgot[i, me] = part[i, h, at]

    def gather(i):
        drain(pgot.at[i], groups - 1, p_sem.at[i, 1])
        pred[i] = (jnp.sum(pgot[i], axis=0) * scale).astype(BF16)
        each_peer(lambda p: q_copy(i, p).start())
        h, at = piece_of(me)
        pall[i, h, at] = pred[i]

    def gathered(i):
        drain(tally, (groups - 1) * piece, q_sem.at[i, 1])
        for h in range(2):
            uo[i, :, h * half_rank : (h + 1) * half_rank] = pall[i, h, 0:width].astype(F32)

    gate_h[...] = (bh[...].astype(F32) * xinp[...].astype(F32)).astype(BF16)
    u_part = mm_tn(gate_h[...], rank_ref[...])
    for h in range(2):
        part[0, h] = u_part[:, h * half_rank : (h + 1) * half_rank]
    part[0, 0, width : width + 8] = mm(jnp.ones((8, rows), BF16), gate_h[...])
    scatter(0)

    for z in range(nz):
        sib_copy(z).wait_recv()

    rank_here = rank_ref[pl.ds(pl.multiple_of(mp * chunk, chunk), chunk), :]

    def shift_of(z, carry):
        ends = uv[z, 0, 0, base:uv_rows].astype(F32)
        first = width - base
        bias_z = ends[first : first + 1] + ends[first + 1 : first + 2] + ends[first + 2 : first + 3]
        up = mm_nt(rank_here[:, 0:half_rank], uv[z, 0, 0]) + mm_nt(
            rank_here[:, half_rank:rank], uv[z, 1, 0]
        )
        shift[z] = up + bias_z + 1.0
        return carry

    lax.fori_loop(0, nz, shift_of, 0)
    for i in range(2):
        swap_copy(i).wait_recv()
        late_copy(i).start()
    gather(0)

    drain(xgot, nz - 1, x_sem.at[1])
    drain(bgot, nz - 1, b_sem.at[1])

    def rank_of(z, total):
        gate = (bgot[z].astype(F32) * xgot[z].astype(F32)).astype(BF16)
        return total[0] + mm(gate, uv[z, 0, 0]), total[1] + mm(gate, uv[z, 1, 0])

    zero = jnp.zeros((chunk, half_rank), F32)
    lo, up = lax.fori_loop(0, nz, rank_of, (zero, zero))
    rr = jnp.concatenate([lo, up], axis=1).astype(BF16)
    rr_all[mp] = rr

    def rr_copy(c, way, step):
        return remote(
            rr_all.at[c],
            rr_all.at[c],
            rr_send.at[way, step],
            rr_recv.at[c],
            column(right if way == 0 else left),
        )

    rr_copy(mp, 0, 0).start()
    rr_copy(mp, 1, 0).start()

    def rr_ring(step):
        came = lax.rem(mp + nz - step, nz)
        rr_copy(came, 0, step - 1).wait_recv()

        @pl.when(step < half_ring)
        def _():
            rr_copy(came, 0, step).start()
            other = lax.rem(mp + step, nz)
            rr_copy(other, 1, step - 1).wait_recv()

            @pl.when(step < half_ring - 1)
            def _():
                rr_copy(other, 1, step).start()

    def input_of(z, carry):
        igp[z] = bgot[z].astype(F32) * shift[z] + (
            mm_nt(rr[:, 0:half_rank], uv[z, 0, 1]) + mm_nt(rr[:, half_rank:rank], uv[z, 1, 1])
        )
        return carry

    for i in range(2):
        late_copy(i).wait_recv()
    lax.fori_loop(0, nz // 2, input_of, 0)
    rr_ring(1)
    lax.fori_loop(nz // 2, nz, input_of, 0)
    rr_ring(2)
    igs[0] = jnp.zeros((chunk, EMB), BF16)
    for t in range(1, igs.shape[0]):
        pieces, at = [], t * EMB
        while at < (t + 1) * EMB:
            z, first = at // width, at % width
            stop = min(width, first + (t + 1) * EMB - at)
            pieces.append(igp[z][:, first:stop])
            at += stop - first
        igs[t] = jnp.concatenate(pieces, axis=1).astype(BF16)

    def t_copy(z):
        return remote(s5.at[z], tgot.at[mp], t_sem.at[0], t_sem.at[1], column(z))

    def fill(z, carry):
        for k in range(slots):
            s5[z, k] = igs[inv_ref[z * slots + k]]
        return carry

    lax.fori_loop(0, nz, fill, 0)
    sent = 0
    for step in range(3, half_ring + 1):
        rr_ring(step)
        upto = nz - 1 if step == half_ring else min(nz - 1, T_SENT[step - 3])
        for o in range(sent + 1, upto + 1):
            t_copy(lax.rem(mp + ((o + 1) // 2 if o % 2 else nz - o // 2), nz)).start()
        sent = upto
    tgot[mp] = s5[mp]

    v_part = mm(xin_t[...], rr_all[...].reshape(rows, rank))
    for h in range(2):
        part[1, h] = v_part[:, h * half_rank : (h + 1) * half_rank]
    scatter(1)
    gathered(0)
    bo[...] = pall[0, 0, width : width + 8].astype(F32)
    stores[1].start()
    stores[3].start()
    gather(1)

    drain(tgot, nz - 1, t_sem.at[1])
    for k in range(slots):
        values = tgot[:, k].reshape(rows, EMB)
        tab_out[k] = (mm(hot[k], values) * scale).astype(BF16)
    stores[4].start()
    gathered(1)
    stores[2].start()

    drain(send, groups - 1, a_send.at[0])
    drain(rsend, groups - 1, r_sem.at[0])
    drain(xgot, nz - 1, x_sem.at[0])
    drain(bgot, nz - 1, b_sem.at[0])
    drain(s5, nz - 1, t_sem.at[0])
    for i in range(2):
        drain(pgot.at[i], groups - 1, p_sem.at[i, 0])
        drain(tally, (groups - 1) * piece, q_sem.at[i, 0])
        swap_copy(i).wait_send()
        late_copy(i).wait_send()
    for z in range(nz):
        sib_copy(z).wait_send()
    for step in range(half_ring):
        uv_copy(mp, 0, step).wait_send()
        rr_copy(mp, 0, step).wait_send()
        if step < half_ring - 1:
            uv_copy(mp, 1, step).wait_send()
            rr_copy(mp, 1, step).wait_send()
    for store in stores:
        store.wait()


def hand_over(wg, u, v, b, table, wg_out, u_out, v_out, b_out, table_out, sems):
    pairs = [(wg, wg_out), (u, u_out), (v, v_out), (table, table_out)]
    copies = [pltpu.make_async_copy(a, c, sems.at[i]) for i, (a, c) in enumerate(pairs)]
    for copy in copies:
        copy.start()
    b_out[...] = b[0:1, 0 : b_out.shape[1]]
    for copy in copies:
        copy.wait()


def on_device(
    cross_in,
    rank_act,
    tower_cot,
    tenant_ids,
    sparse_ids,
    table_slot,
    cross_u,
    cross_v,
    cross_bias,
    tower_w,
):
    nd, nt, nz = lax.axis_size("dp"), lax.axis_size("tenant"), lax.axis_size("mp")
    groups = nd * nt
    rows, width = cross_in.shape
    rank, hid = rank_act.shape[1], tower_cot.shape[1]
    tables = table_slot.shape[0]
    slots = (tables + nz - 1) // nz
    cap = (5 * rows + 4 * groups - 1) // (4 * groups)
    chunk = rows // nz
    half_ring = nz // 2
    scale = 1.0 / math.sqrt(rows * groups)

    anywhere = pl.BlockSpec(memory_space=pl.ANY)
    smem = pl.BlockSpec(memory_space=pltpu.SMEM)
    sem = pltpu.SemaphoreType.DMA

    def bf(*shape):
        return pltpu.VMEM(shape, BF16)

    def ff(*shape):
        return pltpu.VMEM(shape, F32)

    out = pl.pallas_call(
        functools.partial(fused, nd, nt, nz, cap, scale),
        out_shape=(
            jax.ShapeDtypeStruct((width, hid), BF16),
            jax.ShapeDtypeStruct((width, rank), F32),
            jax.ShapeDtypeStruct((width, rank), F32),
            jax.ShapeDtypeStruct((8, WIDE), F32),
            jax.ShapeDtypeStruct((slots, VOCAB, EMB), BF16),
        ),
        in_specs=[smem] + [anywhere] * 9,
        out_specs=(anywhere,) * 5,
        scratch_shapes=[
            pltpu.VMEM((1, rows), jnp.int32),
            bf(width, rows),
            bf(width, rank),
            bf(rows, rank),
            ff(1, width),
            bf(rows, hid),
            bf(width, rank),
            bf(width, hid),
            pltpu.VMEM((tables, rows), jnp.int32),
            bf(width, hid),
            bf(slots, VOCAB, EMB),
            pltpu.SMEM((nz * slots,), jnp.int32),
            sem((9,)),
            sem((5,)),
            ff(2, width, rank),
            ff(8, WIDE),
            bf(nz, 2, 2, WIDE, rank // 2),
            bf(2, WIDE, rank // 2),
            bf(2, WIDE, rank // 2),
            bf(WIDE, rows),
            bf(rows, WIDE),
            bf(rows, WIDE),
            bf(WIDE, hid),
            pltpu.VMEM((8, rows), jnp.int32),
            bf(rows, groups * cap),
            bf(groups, 2 * cap, hid // 2 + 128),
            bf(groups, 2 * cap, hid // 2 + 128),
            bf(groups * cap, hid),
            bf(groups * cap, WIDE),
            bf(groups, 2 * cap, 128),
            bf(groups, 2 * cap, 128),
            bf(groups * cap, WIDE),
            bf(rows, WIDE),
            bf(rows, WIDE),
            bf(nz, chunk, WIDE),
            bf(nz, chunk, WIDE),
            ff(nz, chunk, WIDE),
            bf(nz, chunk, rank),
            ff(nz, chunk, WIDE),
            bf(tables + 1, chunk, EMB),
            bf(nz, slots, chunk, EMB),
            bf(nz, slots, chunk, EMB),
            bf(slots, VOCAB, rows),
            ff(2, 2, WIDE, WIDE),
            ff(2, groups, 2 * WIDE // groups, WIDE),
            bf(2, 2 * WIDE // groups, WIDE),
            bf(2, 2, WIDE, WIDE),
            bf((groups - 1) * 2 * WIDE // groups, WIDE),
            sem((2,)),
            sem((nt // 2,)),
            sem((2,)),
            sem((2,)),
            sem((2,)),
            sem((2, 2, half_ring)),
            sem((2, nz)),
            sem((2, nz)),
            sem((2, nz)),
            sem((2,)),
            sem((2,)),
            sem((2,)),
            sem((2,)),
            sem((2, half_ring)),
            sem((nz,)),
            sem((2,)),
            sem((2, 2)),
            sem((2, 2)),
        ],
        compiler_params=pltpu.CompilerParams(
            collective_id=0, has_side_effects=True, vmem_limit_bytes=60 * 2**20
        ),
    )(
        table_slot,
        tenant_ids.T,
        cross_in.T,
        cross_u,
        rank_act,
        cross_bias[None, :],
        tower_cot,
        cross_v,
        tower_w[0],
        sparse_ids.T,
    )
    vmem = pl.BlockSpec(memory_space=pltpu.VMEM)
    wgrad, u_total, v_total, b_total, table = pl.pallas_call(
        hand_over,
        out_shape=tuple(
            jax.ShapeDtypeStruct((1, width) if i == 3 else x.shape, x.dtype)
            for i, x in enumerate(out)
        ),
        in_specs=[vmem] * 5,
        out_specs=(anywhere, anywhere, anywhere, vmem, anywhere),
        scratch_shapes=[sem((4,))],
    )(*out)
    return wgrad[None], u_total, v_total, b_total[0], table[None]


def solution(mesh):
    return jax.shard_map(
        on_device,
        mesh=mesh,
        in_specs=(
            P(("dp", "tenant"), "mp"),
            P(("dp", "tenant"), None),
            P(("dp", "tenant"), None),
            P(("dp", "tenant"), None),
            P(("dp", "tenant"), None),
            P(),
            P("mp", None),
            P("mp", None),
            P("mp"),
            P(("dp", "tenant"), "mp", None),
        ),
        out_specs=(
            P(("dp", "tenant"), "mp", None),
            P("mp", None),
            P("mp", None),
            P("mp"),
            P(("dp", "tenant"), "mp", None, None),
        ),
        check_vma=False,
    )
```

```python
import functools
import math

import jax
import jax.numpy as jnp
from jax import lax
from jax.experimental import pallas as pl
from jax.experimental.pallas import tpu as pltpu
from jax.sharding import PartitionSpec as P

EMB = 128
VOCAB = 1024
T_SENT = (2, 4, 6, 8, 8)
WIDE = 256
MESH = pl.DeviceIdType.MESH
F32 = jnp.float32
BF16 = jnp.bfloat16


def mm(a, b):
    return jnp.dot(a, b, preferred_element_type=F32)


def mm_nt(a, b):
    return lax.dot_general(a, b, (((1,), (1,)), ((), ())), preferred_element_type=F32)


def mm_tn(a, b):
    return lax.dot_general(a, b, (((0,), (0,)), ((), ())), preferred_element_type=F32)


def fused(
    nd,
    nt,
    nz,
    cap,
    scale,
    slot_ref,
    tenant_hbm,
    xin_hbm,
    u_hbm,
    rank_hbm,
    bias_hbm,
    cot_hbm,
    v_hbm,
    w_hbm,
    ids_hbm,
    wg_hbm,
    u_out_hbm,
    v_out_hbm,
    b_out_hbm,
    tab_hbm,
    tenant_ref,
    xin_ref,
    u_ref,
    rank_ref,
    bias_ref,
    cot_ref,
    v_ref,
    w_ref,
    ids_ref,
    wg_out,
    tab_out,
    inv_ref,
    in_sem,
    out_sem,
    uo,
    bo,
    uv,
    up,
    vp,
    xin_t,
    xinp,
    crp,
    wp,
    tgt,
    perm_t,
    send,
    got,
    cotr,
    crr,
    rsend,
    rgot,
    backb,
    bh,
    gate_h,
    xgot,
    bgot,
    shift,
    rr_all,
    igp,
    igs,
    s5,
    tgot,
    hot,
    part,
    pgot,
    pred,
    pall,
    tally,
    a_send,
    a_recv,
    r_sem,
    x_sem,
    b_sem,
    uv_send,
    uv_recv,
    sib_send,
    sib_recv,
    swap_send,
    swap_recv,
    late_send,
    late_recv,
    rr_send,
    rr_recv,
    t_sem,
    p_sem,
    q_sem,
):
    groups = nd * nt
    width, rows = xin_ref.shape
    rank = rank_ref.shape[1]
    half_rank = rank // 2
    hid = cot_ref.shape[1]
    half_hid = hid // 2
    chunk = rows // nz
    block = nt * cap
    uv_rows = (width + 3 + 15) // 16 * 16
    base = width // 16 * 16
    piece = 2 * WIDE // groups
    per_half = groups // 2
    slots = tab_out.shape[0]

    dp = lax.axis_index("dp")
    tn = lax.axis_index("tenant")
    mp = lax.axis_index("mp")
    me = dp * nt + tn
    core = lax.rem(tn, 2)
    across = tn // 2
    nx = nt // 2

    def partner(o):
        k, a, c = o // (2 * nd), lax.rem(nd - lax.rem(o // 2, nd), nd), lax.rem(o, 2)
        there = lax.rem(across + a + k, nx)
        return lax.rem(dp + a, nd) * nt + 2 * there + lax.rem(core + c, 2)

    def plane(peer):
        return (peer // nt, lax.rem(peer, nt), mp)

    def column(z):
        return (dp, tn, z)

    def remote(src, dst, ssem, rsem, device):
        return pltpu.make_async_remote_copy(
            src_ref=src,
            dst_ref=dst,
            send_sem=ssem,
            recv_sem=rsem,
            device_id=device,
            device_id_type=MESH,
        )

    pairs = [
        (tenant_hbm, tenant_ref),
        (xin_hbm, xin_ref),
        (u_hbm, u_ref),
        (rank_hbm, rank_ref),
        (bias_hbm, bias_ref),
        (cot_hbm, cot_ref),
        (v_hbm, v_ref),
        (w_hbm, w_ref),
        (ids_hbm, ids_ref),
    ]
    loads = [pltpu.make_async_copy(a, b, in_sem.at[i]) for i, (a, b) in enumerate(pairs)]
    for load in loads:
        load.start()

    uv[:, :, 0, uv_rows:, :] = jnp.zeros((nz, 2, WIDE - uv_rows, half_rank), BF16)

    barrier = pltpu.get_barrier_semaphore()

    def greet_plane(o, carry):
        pl.semaphore_signal(barrier, inc=1, device_id=plane(lax.rem(me + o, groups)), device_id_type=MESH)
        return carry

    def greet_column(o, carry):
        pl.semaphore_signal(barrier, inc=1, device_id=column(lax.rem(mp + o, nz)), device_id_type=MESH)
        return carry

    lax.fori_loop(1, groups, greet_plane, 0)
    lax.fori_loop(1, nz, greet_column, 0)

    for load in loads[:5]:
        load.wait()

    bias = jnp.concatenate([bias_ref[...], jnp.zeros((1, WIDE - width), F32)], axis=1)
    hi = bias.astype(BF16).astype(F32)
    mid = (bias - hi).astype(BF16).astype(F32)
    low = bias - hi - mid
    bias_rows = [hi, mid, low, jnp.zeros((WIDE - width - 3, WIDE), F32)]
    for h in range(2):
        cols = slice(h * half_rank, (h + 1) * half_rank)
        up[h, 0:base] = u_ref[0:base, cols]
        tail = bias_rows
        if base < width:
            tail = [u_ref[base:width, cols].astype(F32)] + bias_rows
        up[h, base:WIDE] = jnp.concatenate(tail, axis=0).astype(BF16)
    whole = (width - 1) // 16 * 16

    def padded(ref):
        ends = ref[whole:width].astype(F32)
        ends = jnp.concatenate([ends, jnp.zeros((WIDE - width, ref.shape[1]), F32)], axis=0)
        return ends.astype(BF16)

    xin_t[0:whole] = xin_ref[0:whole]
    xin_t[whole:WIDE] = padded(xin_ref)
    xinp[...] = jnp.transpose(xin_t[...])

    tenant = tenant_ref[...]
    member = lax.broadcasted_iota(jnp.int32, (groups, rows), 0) == tenant
    earlier = lax.broadcasted_iota(jnp.int32, (rows, rows), 0) < lax.broadcasted_iota(
        jnp.int32, (rows, rows), 1
    )
    before = mm(member.astype(F32).astype(BF16), earlier.astype(F32).astype(BF16))
    position = jnp.sum(jnp.where(member, before, 0.0), axis=0, keepdims=True)
    target = tenant * cap + position.astype(jnp.int32)
    tgt[...] = jnp.broadcast_to(target, tgt.shape)

    pl.semaphore_wait(barrier, groups - 1 + nz - 1)

    right, left = lax.rem(mp + 1, nz), lax.rem(mp + nz - 1, nz)
    sibling = (dp, tn + 1 - 2 * core, mp)
    beside = (dp, lax.rem(across + 1, 2) * 2 + across // 2 * 4 + core, mp)
    above = (dp // 2 * 2 + 1 - lax.rem(dp, 2), tn, mp)
    half_ring = nz // 2

    half_rows = uv_rows // 2
    even = lax.rem(across + dp, 2)
    mine = pl.ds(pl.multiple_of(even * half_rows, half_rows), half_rows)
    others = pl.ds(pl.multiple_of((1 - even) * half_rows, half_rows), half_rows)

    class Both:
        def __init__(self, copies):
            self.copies = copies

        def start(self):
            for copy in self.copies:
                copy.start()

        def wait_recv(self):
            for copy in self.copies:
                copy.wait_recv()

        def wait_send(self):
            for copy in self.copies:
                copy.wait_send()

    def parts(c):
        return uv.at[c, core, 0, 0:uv_rows], uv.at[c, core, 1, mine]

    def uv_copy(c, way, step):
        to = column(right if way == 0 else left)
        return Both(
            [remote(x, x, uv_send.at[i, way, step], uv_recv.at[i, c], to) for i, x in enumerate(parts(c))]
        )

    def sib_copy(c):
        return Both(
            [remote(x, x, sib_send.at[i, c], sib_recv.at[i, c], sibling) for i, x in enumerate(parts(c))]
        )

    def swap_copy(i):
        spot = uv.at[i * half_ring : (i + 1) * half_ring, core, 1, mine]
        return remote(spot, spot, swap_send.at[i], swap_recv.at[i], above if i else beside)

    def late_copy(i):
        spot = uv.at[i * half_ring : (i + 1) * half_ring, core, 1, others]
        return remote(spot, spot, late_send.at[i], late_recv.at[i], sibling)

    def uv_ring(step):
        came = lax.rem(mp + nz - step, nz)
        uv_copy(came, 0, step - 1).wait_recv()

        @pl.when(step < half_ring)
        def _():
            uv_copy(came, 0, step).start()

        sib_copy(came).start()

        @pl.when(step < half_ring)
        def _():
            other = lax.rem(mp + step, nz)
            uv_copy(other, 1, step - 1).wait_recv()

            @pl.when(step < half_ring - 1)
            def _():
                uv_copy(other, 1, step).start()

            sib_copy(other).start()

    loads[6].wait()
    for h in range(2):
        vp[h, 0:whole] = v_ref[0:whole, h * half_rank : (h + 1) * half_rank]
        vp[h, whole:WIDE] = padded(v_ref)[:, h * half_rank : (h + 1) * half_rank]
    uv[mp, core, 0, 0:uv_rows] = up[core, 0:uv_rows]
    uv[mp, core, 1, mine] = vp[core, mine]
    uv_copy(mp, 0, 0).start()
    uv_copy(mp, 1, 0).start()
    sib_copy(mp).start()

    rank_up = mm_nt(rank_ref[:, 0:half_rank], up[0]) + mm_nt(rank_ref[:, half_rank:rank], up[1])
    wide = xinp[...].astype(F32)
    crp[...] = (wide * (rank_up + bias) + wide).astype(BF16)

    loads[5].wait()

    def drain(ref, count, sem):
        spot = ref.at[pl.ds(0, count)]
        pltpu.make_async_copy(spot, spot, sem).wait()

    def a_copy(peer, k):
        return remote(send.at[peer], got.at[me], a_send.at[0], a_recv.at[k], plane(peer))

    def tenants_of(k, way):
        first = []
        for a in range(nd):
            up = lax.rem(dp + nd + way * a, nd)
            there = lax.rem(across + 2 * nx + way * lax.rem(a + k, nx), nx)
            first.append(up * nt + 2 * there)
        return first

    def bucket(k, carry):
        firsts = tenants_of(k, 1)
        spots = lax.broadcasted_iota(jnp.int32, (2 * cap, rows), 0)
        chosen = jnp.concatenate([spots + first * cap for first in firsts], axis=0) == tgt[0:1, :]
        chosen = chosen.astype(F32).astype(BF16)
        cots = mm(chosen, cot_ref[...])
        crossed = mm(chosen, crp[...])
        for j in range(2 * nd):
            s = slice(j * cap, (j + 1) * cap)
            send[firsts[j // 2] + j % 2] = jnp.concatenate(
                [
                    jnp.concatenate([cots[s, 0:half_hid], crossed[s, 0:128]], axis=1),
                    jnp.concatenate([cots[s, half_hid:hid], crossed[s, 128:WIDE]], axis=1),
                ],
                axis=0,
            ).astype(BF16)

        def start(o, inner):
            peer = partner(k * 2 * nd + o)

            @pl.when(peer != me)
            def _():
                a_copy(peer, k).start()

            return inner

        lax.fori_loop(0, 2 * nd, start, 0)
        return carry

    lax.fori_loop(0, nx, bucket, 0)
    got[me] = send[me]

    target_col = jnp.transpose(tgt[...].astype(F32))[:, 0:1].astype(jnp.int32)
    perm_t[...] = (
        (lax.broadcasted_iota(jnp.int32, perm_t.shape, 1) == target_col).astype(F32).astype(BF16)
    )

    uv_ring(1)
    loads[7].wait()
    wp[0:whole] = w_ref[0:whole]
    wp[whole:WIDE] = padded(w_ref)
    uv_ring(2)

    tables = slot_ref.shape[0]

    def invert(slot, carry):
        number = jnp.int32(0)
        for t in range(tables):
            number = jnp.where(slot_ref[t] == slot, t + 1, number)
        inv_ref[slot] = number
        return carry

    lax.fori_loop(0, nz * slots, invert, 0)
    loads[8].wait()
    for k in range(slots):
        table = inv_ref[mp * slots + k] - 1
        ids = jnp.sum(
            jnp.where(lax.broadcasted_iota(jnp.int32, ids_ref.shape, 0) == table, ids_ref[...], 0),
            axis=0,
            keepdims=True,
        )
        hot[k] = (lax.broadcasted_iota(jnp.int32, (VOCAB, rows), 0) == ids).astype(F32).astype(BF16)

    uv_ring(3)

    def x_copy(z):
        here = pl.ds(pl.multiple_of(z * chunk, chunk), chunk)
        return remote(xinp.at[here], xgot.at[mp], x_sem.at[0], x_sem.at[1], column(z))

    def each_z(body):
        def run(o, carry):
            step = (o + 1) // 2
            body(lax.rem(mp + jnp.where(lax.rem(o, 2) == 1, step, nz - step), nz))
            return carry

        lax.fori_loop(1, nz, run, 0)

    def each_peer(body):
        def run(o, carry):
            body(partner(o))
            return carry

        lax.fori_loop(1, groups, run, 0)

    xgot[mp] = xinp[pl.ds(pl.multiple_of(mp * chunk, chunk), chunk)]

    def r_copy(peer):
        return remote(rsend.at[peer], rgot.at[me], r_sem.at[0], r_sem.at[1], plane(peer))

    for step in range(4, half_ring - 1):
        uv_ring(step)
        if step == half_ring - 3:
            each_z(lambda z: x_copy(z).start())
    if half_ring < 7:
        each_z(lambda z: x_copy(z).start())

    def owner(k, carry):
        firsts = tenants_of(k, -1)

        @pl.when(k == 0)
        def _():
            drain(got, 2 * nd - 1, a_recv.at[0])

        @pl.when(k > 0)
        def _():
            drain(got, 2 * nd, a_recv.at[k])

        cots, crossed = [], []
        for first in firsts:
            for j in range(2):
                blk = got[first + j].astype(F32)
                cots.append(jnp.concatenate([blk[0:cap, 0:half_hid], blk[cap:, 0:half_hid]], axis=1))
                crossed.append(jnp.concatenate([blk[0:cap, half_hid:], blk[cap:, half_hid:]], axis=1))
        cots = jnp.concatenate(cots, axis=0).astype(BF16)
        at = pl.ds(pl.multiple_of(k * 2 * nd * cap, 2 * nd * cap), 2 * nd * cap)
        cotr[at] = cots
        crr[at] = jnp.concatenate(crossed, axis=0).astype(BF16)
        back = mm_nt(cots, wp[...])
        for j in range(2 * nd):
            s = slice(j * cap, (j + 1) * cap)
            rsend[firsts[j // 2] + j % 2] = jnp.concatenate(
                [back[s, 0:128], back[s, 128:WIDE]], axis=0
            ).astype(BF16)
        for first in firsts:
            for j in range(2):

                @pl.when(first + j != me)
                def _():
                    r_copy(first + j).start()

        return carry

    lax.fori_loop(0, nx, owner, 0)
    rgot[me] = rsend[me]
    if half_ring > 4:
        uv_ring(half_ring - 1)

    wgrad = mm_tn(crr[...], cotr[...])
    wg_out[...] = (wgrad[0:width] * scale).astype(BF16)
    stores = [
        pltpu.make_async_copy(wg_out, wg_hbm, out_sem.at[0]),
        pltpu.make_async_copy(uo.at[0], u_out_hbm, out_sem.at[1]),
        pltpu.make_async_copy(uo.at[1], v_out_hbm, out_sem.at[2]),
        pltpu.make_async_copy(bo, b_out_hbm, out_sem.at[3]),
        pltpu.make_async_copy(tab_out, tab_hbm, out_sem.at[4]),
    ]
    stores[0].start()

    drain(rgot, groups - 1, r_sem.at[1])

    def unpack(t, carry):
        pair = []
        for j in range(2):
            blk = rgot[2 * t + j].astype(F32)
            pair.append(jnp.concatenate([blk[0:cap], blk[cap:]], axis=1))
        backb[pl.ds(pl.multiple_of(t * 2 * cap, 2 * cap), 2 * cap)] = jnp.concatenate(
            pair, axis=0
        ).astype(BF16)
        return carry

    lax.fori_loop(0, groups // 2, unpack, 0)
    bh[...] = mm(perm_t[...], backb[...]).astype(BF16)

    def b_copy(z):
        here = pl.ds(pl.multiple_of(z * chunk, chunk), chunk)
        return remote(bh.at[here], bgot.at[mp], b_sem.at[0], b_sem.at[1], column(z))

    each_z(lambda z: b_copy(z).start())
    bgot[mp] = bh[pl.ds(pl.multiple_of(mp * chunk, chunk), chunk)]

    def piece_of(peer):
        return peer // per_half, pl.ds(pl.multiple_of(lax.rem(peer, per_half) * piece, piece), piece)

    def p_copy(i, peer):
        h, at = piece_of(peer)
        return remote(part.at[i, h, at], pgot.at[i, me], p_sem.at[i, 0], p_sem.at[i, 1], plane(peer))

    def q_copy(i, peer):
        h, at = piece_of(me)
        return remote(pred.at[i], pall.at[i, h, at], q_sem.at[i, 0], q_sem.at[i, 1], plane(peer))

    def scatter(i):
        each_peer(lambda p: p_copy(i, p).start())
        h, at = piece_of(me)
        pgot[i, me] = part[i, h, at]

    def gather(i):
        drain(pgot.at[i], groups - 1, p_sem.at[i, 1])
        pred[i] = (jnp.sum(pgot[i], axis=0) * scale).astype(BF16)
        each_peer(lambda p: q_copy(i, p).start())
        h, at = piece_of(me)
        pall[i, h, at] = pred[i]

    def gathered(i):
        drain(tally, (groups - 1) * piece, q_sem.at[i, 1])
        for h in range(2):
            uo[i, :, h * half_rank : (h + 1) * half_rank] = pall[i, h, 0:width].astype(F32)

    gate_h[...] = (bh[...].astype(F32) * xinp[...].astype(F32)).astype(BF16)
    u_part = mm_tn(gate_h[...], rank_ref[...])
    for h in range(2):
        part[0, h] = u_part[:, h * half_rank : (h + 1) * half_rank]
    part[0, 0, width : width + 8] = mm(jnp.ones((8, rows), BF16), gate_h[...])
    scatter(0)

    uv_ring(half_ring)
    for i in range(2):
        swap_copy(i).start()
    for z in range(nz):
        sib_copy(z).wait_recv()

    rank_here = rank_ref[pl.ds(pl.multiple_of(mp * chunk, chunk), chunk), :]

    def shift_of(z, carry):
        ends = uv[z, 0, 0, base:uv_rows].astype(F32)
        first = width - base
        bias_z = ends[first : first + 1] + ends[first + 1 : first + 2] + ends[first + 2 : first + 3]
        up = mm_nt(rank_here[:, 0:half_rank], uv[z, 0, 0]) + mm_nt(
            rank_here[:, half_rank:rank], uv[z, 1, 0]
        )
        shift[z] = up + bias_z + 1.0
        return carry

    lax.fori_loop(0, nz, shift_of, 0)
    for i in range(2):
        swap_copy(i).wait_recv()
        late_copy(i).start()
    gather(0)

    drain(xgot, nz - 1, x_sem.at[1])
    drain(bgot, nz - 1, b_sem.at[1])

    def rank_of(z, total):
        gate = (bgot[z].astype(F32) * xgot[z].astype(F32)).astype(BF16)
        return total[0] + mm(gate, uv[z, 0, 0]), total[1] + mm(gate, uv[z, 1, 0])

    zero = jnp.zeros((chunk, half_rank), F32)
    lo, up = lax.fori_loop(0, nz, rank_of, (zero, zero))
    rr = jnp.concatenate([lo, up], axis=1).astype(BF16)
    rr_all[mp] = rr

    def rr_copy(c, way, step, i):
        spot = rr_all.at[c, pl.ds(i * (chunk // 2), chunk // 2)]
        to = column(right if way == 0 else left)
        return remote(spot, spot, rr_send.at[i, way, step], rr_recv.at[i, c], to)

    for i in range(2):
        rr_copy(mp, 0, 0, i).start()
        rr_copy(mp, 1, 0, i).start()

    def rr_ring(step):
        came = lax.rem(mp + nz - step, nz)
        other = lax.rem(mp + step, nz)
        for i in range(2):
            rr_copy(came, 0, step - 1, i).wait_recv()
            if step < half_ring:
                rr_copy(came, 0, step, i).start()
                rr_copy(other, 1, step - 1, i).wait_recv()
            if step < half_ring - 1:
                rr_copy(other, 1, step, i).start()

    def input_of(z, carry):
        igp[z] = bgot[z].astype(F32) * shift[z] + (
            mm_nt(rr[:, 0:half_rank], uv[z, 0, 1]) + mm_nt(rr[:, half_rank:rank], uv[z, 1, 1])
        )
        return carry

    for i in range(2):
        late_copy(i).wait_recv()
    lax.fori_loop(0, nz // 2, input_of, 0)
    rr_ring(1)
    lax.fori_loop(nz // 2, nz, input_of, 0)
    rr_ring(2)
    igs[0] = jnp.zeros((chunk, EMB), BF16)
    for t in range(1, igs.shape[0]):
        pieces, at = [], t * EMB
        while at < (t + 1) * EMB:
            z, first = at // width, at % width
            stop = min(width, first + (t + 1) * EMB - at)
            pieces.append(igp[z][:, first:stop])
            at += stop - first
        igs[t] = jnp.concatenate(pieces, axis=1).astype(BF16)

    def t_copy(z):
        return remote(s5.at[z], tgot.at[mp], t_sem.at[0], t_sem.at[1], column(z))

    def fill(z, carry):
        for k in range(slots):
            s5[z, k] = igs[inv_ref[z * slots + k]]
        return carry

    lax.fori_loop(0, nz, fill, 0)
    sent = 0
    for step in range(3, half_ring + 1):
        rr_ring(step)
        upto = nz - 1 if step == half_ring else min(nz - 1, T_SENT[step - 3])
        for o in range(sent + 1, upto + 1):
            t_copy(lax.rem(mp + ((o + 1) // 2 if o % 2 else nz - o // 2), nz)).start()
        sent = upto
    tgot[mp] = s5[mp]

    v_part = mm(xin_t[...], rr_all[...].reshape(rows, rank))
    for h in range(2):
        part[1, h] = v_part[:, h * half_rank : (h + 1) * half_rank]
    scatter(1)
    gathered(0)
    bo[...] = pall[0, 0, width : width + 8].astype(F32)
    stores[1].start()
    stores[3].start()
    gather(1)

    drain(tgot, nz - 1, t_sem.at[1])
    for k in range(slots):
        values = tgot[:, k].reshape(rows, EMB)
        tab_out[k] = (mm(hot[k], values) * scale).astype(BF16)
    stores[4].start()
    gathered(1)
    stores[2].start()

    drain(send, groups - 1, a_send.at[0])
    drain(rsend, groups - 1, r_sem.at[0])
    drain(xgot, nz - 1, x_sem.at[0])
    drain(bgot, nz - 1, b_sem.at[0])
    drain(s5, nz - 1, t_sem.at[0])
    for i in range(2):
        drain(pgot.at[i], groups - 1, p_sem.at[i, 0])
        drain(tally, (groups - 1) * piece, q_sem.at[i, 0])
        swap_copy(i).wait_send()
        late_copy(i).wait_send()
    for z in range(nz):
        sib_copy(z).wait_send()
    for step in range(half_ring):
        uv_copy(mp, 0, step).wait_send()
        for i in range(2):
            rr_copy(mp, 0, step, i).wait_send()
        if step < half_ring - 1:
            uv_copy(mp, 1, step).wait_send()
            for i in range(2):
                rr_copy(mp, 1, step, i).wait_send()
    for store in stores:
        store.wait()


def hand_over(wg, u, v, b, table, wg_out, u_out, v_out, b_out, table_out, sems):
    pairs = [(wg, wg_out), (u, u_out), (v, v_out), (table, table_out)]
    copies = [pltpu.make_async_copy(a, c, sems.at[i]) for i, (a, c) in enumerate(pairs)]
    for copy in copies:
        copy.start()
    b_out[...] = b[0:1, 0 : b_out.shape[1]]
    for copy in copies:
        copy.wait()


def on_device(
    cross_in,
    rank_act,
    tower_cot,
    tenant_ids,
    sparse_ids,
    table_slot,
    cross_u,
    cross_v,
    cross_bias,
    tower_w,
):
    nd, nt, nz = lax.axis_size("dp"), lax.axis_size("tenant"), lax.axis_size("mp")
    groups = nd * nt
    rows, width = cross_in.shape
    rank, hid = rank_act.shape[1], tower_cot.shape[1]
    tables = table_slot.shape[0]
    slots = (tables + nz - 1) // nz
    cap = (5 * rows + 4 * groups - 1) // (4 * groups)
    chunk = rows // nz
    half_ring = nz // 2
    scale = 1.0 / math.sqrt(rows * groups)

    anywhere = pl.BlockSpec(memory_space=pl.ANY)
    smem = pl.BlockSpec(memory_space=pltpu.SMEM)
    sem = pltpu.SemaphoreType.DMA

    def bf(*shape):
        return pltpu.VMEM(shape, BF16)

    def ff(*shape):
        return pltpu.VMEM(shape, F32)

    out = pl.pallas_call(
        functools.partial(fused, nd, nt, nz, cap, scale),
        out_shape=(
            jax.ShapeDtypeStruct((width, hid), BF16),
            jax.ShapeDtypeStruct((width, rank), F32),
            jax.ShapeDtypeStruct((width, rank), F32),
            jax.ShapeDtypeStruct((8, WIDE), F32),
            jax.ShapeDtypeStruct((slots, VOCAB, EMB), BF16),
        ),
        in_specs=[smem] + [anywhere] * 9,
        out_specs=(anywhere,) * 5,
        scratch_shapes=[
            pltpu.VMEM((1, rows), jnp.int32),
            bf(width, rows),
            bf(width, rank),
            bf(rows, rank),
            ff(1, width),
            bf(rows, hid),
            bf(width, rank),
            bf(width, hid),
            pltpu.VMEM((tables, rows), jnp.int32),
            bf(width, hid),
            bf(slots, VOCAB, EMB),
            pltpu.SMEM((nz * slots,), jnp.int32),
            sem((9,)),
            sem((5,)),
            ff(2, width, rank),
            ff(8, WIDE),
            bf(nz, 2, 2, WIDE, rank // 2),
            bf(2, WIDE, rank // 2),
            bf(2, WIDE, rank // 2),
            bf(WIDE, rows),
            bf(rows, WIDE),
            bf(rows, WIDE),
            bf(WIDE, hid),
            pltpu.VMEM((8, rows), jnp.int32),
            bf(rows, groups * cap),
            bf(groups, 2 * cap, hid // 2 + 128),
            bf(groups, 2 * cap, hid // 2 + 128),
            bf(groups * cap, hid),
            bf(groups * cap, WIDE),
            bf(groups, 2 * cap, 128),
            bf(groups, 2 * cap, 128),
            bf(groups * cap, WIDE),
            bf(rows, WIDE),
            bf(rows, WIDE),
            bf(nz, chunk, WIDE),
            bf(nz, chunk, WIDE),
            ff(nz, chunk, WIDE),
            bf(nz, chunk, rank),
            ff(nz, chunk, WIDE),
            bf(tables + 1, chunk, EMB),
            bf(nz, slots, chunk, EMB),
            bf(nz, slots, chunk, EMB),
            bf(slots, VOCAB, rows),
            ff(2, 2, WIDE, WIDE),
            ff(2, groups, 2 * WIDE // groups, WIDE),
            bf(2, 2 * WIDE // groups, WIDE),
            bf(2, 2, WIDE, WIDE),
            bf((groups - 1) * 2 * WIDE // groups, WIDE),
            sem((2,)),
            sem((nt // 2,)),
            sem((2,)),
            sem((2,)),
            sem((2,)),
            sem((2, 2, half_ring)),
            sem((2, nz)),
            sem((2, nz)),
            sem((2, nz)),
            sem((2,)),
            sem((2,)),
            sem((2,)),
            sem((2,)),
            sem((2, 2, half_ring)),
            sem((2, nz)),
            sem((2,)),
            sem((2, 2)),
            sem((2, 2)),
        ],
        compiler_params=pltpu.CompilerParams(
            collective_id=0, has_side_effects=True, vmem_limit_bytes=60 * 2**20
        ),
    )(
        table_slot,
        tenant_ids.T,
        cross_in.T,
        cross_u,
        rank_act,
        cross_bias[None, :],
        tower_cot,
        cross_v,
        tower_w[0],
        sparse_ids.T,
    )
    vmem = pl.BlockSpec(memory_space=pltpu.VMEM)
    wgrad, u_total, v_total, b_total, table = pl.pallas_call(
        hand_over,
        out_shape=tuple(
            jax.ShapeDtypeStruct((1, width) if i == 3 else x.shape, x.dtype)
            for i, x in enumerate(out)
        ),
        in_specs=[vmem] * 5,
        out_specs=(anywhere, anywhere, anywhere, vmem, anywhere),
        scratch_shapes=[sem((4,))],
    )(*out)
    return wgrad[None], u_total, v_total, b_total[0], table[None]


def solution(mesh):
    return jax.shard_map(
        on_device,
        mesh=mesh,
        in_specs=(
            P(("dp", "tenant"), "mp"),
            P(("dp", "tenant"), None),
            P(("dp", "tenant"), None),
            P(("dp", "tenant"), None),
            P(("dp", "tenant"), None),
            P(),
            P("mp", None),
            P("mp", None),
            P("mp"),
            P(("dp", "tenant"), "mp", None),
        ),
        out_specs=(
            P(("dp", "tenant"), "mp", None),
            P("mp", None),
            P("mp", None),
            P("mp"),
            P(("dp", "tenant"), "mp", None, None),
        ),
        check_vma=False,
    )
```

```python
import functools
import math

import jax
import jax.numpy as jnp
from jax import lax
from jax.experimental import pallas as pl
from jax.experimental.pallas import tpu as pltpu
from jax.sharding import PartitionSpec as P

EMB = 128
VOCAB = 1024
T_SENT = (0, 2, 4, 4, 6)
WIDE = 256
MESH = pl.DeviceIdType.MESH
F32 = jnp.float32
BF16 = jnp.bfloat16


def mm(a, b):
    return jnp.dot(a, b, preferred_element_type=F32)


def mm_nt(a, b):
    return lax.dot_general(a, b, (((1,), (1,)), ((), ())), preferred_element_type=F32)


def mm_tn(a, b):
    return lax.dot_general(a, b, (((0,), (0,)), ((), ())), preferred_element_type=F32)


def fused(
    nd,
    nt,
    nz,
    cap,
    scale,
    slot_ref,
    tenant_hbm,
    xin_hbm,
    u_hbm,
    rank_hbm,
    bias_hbm,
    cot_hbm,
    v_hbm,
    w_hbm,
    ids_hbm,
    wg_hbm,
    u_out_hbm,
    v_out_hbm,
    b_out_hbm,
    tab_hbm,
    tenant_ref,
    xin_ref,
    u_ref,
    rank_ref,
    bias_ref,
    cot_ref,
    v_ref,
    w_ref,
    ids_ref,
    wg_out,
    tab_out,
    inv_ref,
    in_sem,
    out_sem,
    uo,
    bo,
    uv,
    up,
    vp,
    xin_t,
    xinp,
    crp,
    wp,
    tgt,
    perm_t,
    send,
    got,
    cotr,
    crr,
    rsend,
    rgot,
    backb,
    bh,
    gate_h,
    xgot,
    bgot,
    shift,
    rr_all,
    igp,
    igs,
    s5,
    tgot,
    hot,
    part,
    pgot,
    pred,
    pall,
    tally,
    a_send,
    a_recv,
    r_sem,
    x_sem,
    b_sem,
    uv_send,
    uv_recv,
    sib_send,
    sib_recv,
    swap_send,
    swap_recv,
    late_send,
    late_recv,
    rr_send,
    rr_recv,
    t_sem,
    p_sem,
    q_sem,
):
    groups = nd * nt
    width, rows = xin_ref.shape
    rank = rank_ref.shape[1]
    half_rank = rank // 2
    hid = cot_ref.shape[1]
    half_hid = hid // 2
    chunk = rows // nz
    block = nt * cap
    uv_rows = (width + 3 + 15) // 16 * 16
    base = width // 16 * 16
    piece = 2 * WIDE // groups
    per_half = groups // 2
    slots = tab_out.shape[0]

    dp = lax.axis_index("dp")
    tn = lax.axis_index("tenant")
    mp = lax.axis_index("mp")
    me = dp * nt + tn
    core = lax.rem(tn, 2)
    across = tn // 2
    nx = nt // 2

    def partner(o):
        k, a, c = o // (2 * nd), lax.rem(nd - lax.rem(o // 2, nd), nd), lax.rem(o, 2)
        there = lax.rem(across + a + k, nx)
        return lax.rem(dp + a, nd) * nt + 2 * there + lax.rem(core + c, 2)

    def plane(peer):
        return (peer // nt, lax.rem(peer, nt), mp)

    def column(z):
        return (dp, tn, z)

    def remote(src, dst, ssem, rsem, device):
        return pltpu.make_async_remote_copy(
            src_ref=src,
            dst_ref=dst,
            send_sem=ssem,
            recv_sem=rsem,
            device_id=device,
            device_id_type=MESH,
        )

    pairs = [
        (tenant_hbm, tenant_ref),
        (xin_hbm, xin_ref),
        (u_hbm, u_ref),
        (rank_hbm, rank_ref),
        (bias_hbm, bias_ref),
        (cot_hbm, cot_ref),
        (v_hbm, v_ref),
        (w_hbm, w_ref),
        (ids_hbm, ids_ref),
    ]
    loads = [pltpu.make_async_copy(a, b, in_sem.at[i]) for i, (a, b) in enumerate(pairs)]
    for load in loads:
        load.start()

    uv[:, :, 0, uv_rows:, :] = jnp.zeros((nz, 2, WIDE - uv_rows, half_rank), BF16)

    barrier = pltpu.get_barrier_semaphore()

    def greet_plane(o, carry):
        pl.semaphore_signal(barrier, inc=1, device_id=plane(lax.rem(me + o, groups)), device_id_type=MESH)
        return carry

    def greet_column(o, carry):
        pl.semaphore_signal(barrier, inc=1, device_id=column(lax.rem(mp + o, nz)), device_id_type=MESH)
        return carry

    lax.fori_loop(1, groups, greet_plane, 0)
    lax.fori_loop(1, nz, greet_column, 0)

    for load in loads[:5]:
        load.wait()

    bias = jnp.concatenate([bias_ref[...], jnp.zeros((1, WIDE - width), F32)], axis=1)
    hi = bias.astype(BF16).astype(F32)
    mid = (bias - hi).astype(BF16).astype(F32)
    low = bias - hi - mid
    bias_rows = [hi, mid, low, jnp.zeros((WIDE - width - 3, WIDE), F32)]
    for h in range(2):
        cols = slice(h * half_rank, (h + 1) * half_rank)
        up[h, 0:base] = u_ref[0:base, cols]
        tail = bias_rows
        if base < width:
            tail = [u_ref[base:width, cols].astype(F32)] + bias_rows
        up[h, base:WIDE] = jnp.concatenate(tail, axis=0).astype(BF16)
    whole = (width - 1) // 16 * 16

    def padded(ref):
        ends = ref[whole:width].astype(F32)
        ends = jnp.concatenate([ends, jnp.zeros((WIDE - width, ref.shape[1]), F32)], axis=0)
        return ends.astype(BF16)

    xin_t[0:whole] = xin_ref[0:whole]
    xin_t[whole:WIDE] = padded(xin_ref)
    xinp[...] = jnp.transpose(xin_t[...])

    tenant = tenant_ref[...]
    member = lax.broadcasted_iota(jnp.int32, (groups, rows), 0) == tenant
    earlier = lax.broadcasted_iota(jnp.int32, (rows, rows), 0) < lax.broadcasted_iota(
        jnp.int32, (rows, rows), 1
    )
    before = mm(member.astype(F32).astype(BF16), earlier.astype(F32).astype(BF16))
    position = jnp.sum(jnp.where(member, before, 0.0), axis=0, keepdims=True)
    target = tenant * cap + position.astype(jnp.int32)
    tgt[...] = jnp.broadcast_to(target, tgt.shape)

    pl.semaphore_wait(barrier, groups - 1 + nz - 1)

    right, left = lax.rem(mp + 1, nz), lax.rem(mp + nz - 1, nz)
    sibling = (dp, tn + 1 - 2 * core, mp)
    beside = (dp, lax.rem(across + 1, 2) * 2 + across // 2 * 4 + core, mp)
    above = (dp // 2 * 2 + 1 - lax.rem(dp, 2), tn, mp)
    half_ring = nz // 2

    half_rows = uv_rows // 2
    even = lax.rem(across + dp, 2)
    mine = pl.ds(pl.multiple_of(even * half_rows, half_rows), half_rows)
    others = pl.ds(pl.multiple_of((1 - even) * half_rows, half_rows), half_rows)

    class Both:
        def __init__(self, copies):
            self.copies = copies

        def start(self):
            for copy in self.copies:
                copy.start()

        def wait_recv(self):
            for copy in self.copies:
                copy.wait_recv()

        def wait_send(self):
            for copy in self.copies:
                copy.wait_send()

    def parts(c):
        return uv.at[c, core, 0, 0:uv_rows], uv.at[c, core, 1, mine]

    def uv_copy(c, way, step):
        to = column(right if way == 0 else left)
        return Both(
            [remote(x, x, uv_send.at[i, way, step], uv_recv.at[i, c], to) for i, x in enumerate(parts(c))]
        )

    def sib_copy(c):
        return Both(
            [remote(x, x, sib_send.at[i, c], sib_recv.at[i, c], sibling) for i, x in enumerate(parts(c))]
        )

    def swap_copy(i):
        spot = uv.at[i * half_ring : (i + 1) * half_ring, core, 1, mine]
        return remote(spot, spot, swap_send.at[i], swap_recv.at[i], above if i else beside)

    def late_copy(i):
        spot = uv.at[i * half_ring : (i + 1) * half_ring, core, 1, others]
        return remote(spot, spot, late_send.at[i], late_recv.at[i], sibling)

    def uv_ring(step):
        came = lax.rem(mp + nz - step, nz)
        uv_copy(came, 0, step - 1).wait_recv()

        @pl.when(step < half_ring)
        def _():
            uv_copy(came, 0, step).start()

        sib_copy(came).start()

        @pl.when(step < half_ring)
        def _():
            other = lax.rem(mp + step, nz)
            uv_copy(other, 1, step - 1).wait_recv()

            @pl.when(step < half_ring - 1)
            def _():
                uv_copy(other, 1, step).start()

            sib_copy(other).start()

    loads[6].wait()
    for h in range(2):
        vp[h, 0:whole] = v_ref[0:whole, h * half_rank : (h + 1) * half_rank]
        vp[h, whole:WIDE] = padded(v_ref)[:, h * half_rank : (h + 1) * half_rank]
    uv[mp, core, 0, 0:uv_rows] = up[core, 0:uv_rows]
    uv[mp, core, 1, mine] = vp[core, mine]
    uv_copy(mp, 0, 0).start()
    uv_copy(mp, 1, 0).start()
    sib_copy(mp).start()

    rank_up = mm_nt(rank_ref[:, 0:half_rank], up[0]) + mm_nt(rank_ref[:, half_rank:rank], up[1])
    wide = xinp[...].astype(F32)
    crp[...] = (wide * (rank_up + bias) + wide).astype(BF16)

    loads[5].wait()

    def drain(ref, count, sem):
        spot = ref.at[pl.ds(0, count)]
        pltpu.make_async_copy(spot, spot, sem).wait()

    def a_copy(peer, k):
        return remote(send.at[peer], got.at[me], a_send.at[0], a_recv.at[k], plane(peer))

    def tenants_of(k, way):
        first = []
        for a in range(nd):
            up = lax.rem(dp + nd + way * a, nd)
            there = lax.rem(across + 2 * nx + way * lax.rem(a + k, nx), nx)
            first.append(up * nt + 2 * there)
        return first

    def bucket(k, carry):
        firsts = tenants_of(k, 1)
        spots = lax.broadcasted_iota(jnp.int32, (2 * cap, rows), 0)
        chosen = jnp.concatenate([spots + first * cap for first in firsts], axis=0) == tgt[0:1, :]
        chosen = chosen.astype(F32).astype(BF16)
        cots = mm(chosen, cot_ref[...])
        crossed = mm(chosen, crp[...])
        for j in range(2 * nd):
            s = slice(j * cap, (j + 1) * cap)
            send[firsts[j // 2] + j % 2] = jnp.concatenate(
                [
                    jnp.concatenate([cots[s, 0:half_hid], crossed[s, 0:128]], axis=1),
                    jnp.concatenate([cots[s, half_hid:hid], crossed[s, 128:WIDE]], axis=1),
                ],
                axis=0,
            ).astype(BF16)

        def start(o, inner):
            peer = partner(k * 2 * nd + o)

            @pl.when(peer != me)
            def _():
                a_copy(peer, k).start()

            return inner

        lax.fori_loop(0, 2 * nd, start, 0)
        return carry

    lax.fori_loop(0, nx, bucket, 0)
    got[me] = send[me]

    target_col = jnp.transpose(tgt[...].astype(F32))[:, 0:1].astype(jnp.int32)
    perm_t[...] = (
        (lax.broadcasted_iota(jnp.int32, perm_t.shape, 1) == target_col).astype(F32).astype(BF16)
    )

    uv_ring(1)
    loads[7].wait()
    wp[0:whole] = w_ref[0:whole]
    wp[whole:WIDE] = padded(w_ref)
    uv_ring(2)

    tables = slot_ref.shape[0]

    def invert(slot, carry):
        number = jnp.int32(0)
        for t in range(tables):
            number = jnp.where(slot_ref[t] == slot, t + 1, number)
        inv_ref[slot] = number
        return carry

    lax.fori_loop(0, nz * slots, invert, 0)
    loads[8].wait()
    for k in range(slots):
        table = inv_ref[mp * slots + k] - 1
        ids = jnp.sum(
            jnp.where(lax.broadcasted_iota(jnp.int32, ids_ref.shape, 0) == table, ids_ref[...], 0),
            axis=0,
            keepdims=True,
        )
        hot[k] = (lax.broadcasted_iota(jnp.int32, (VOCAB, rows), 0) == ids).astype(F32).astype(BF16)

    uv_ring(3)

    def x_copy(z):
        here = pl.ds(pl.multiple_of(z * chunk, chunk), chunk)
        return remote(xinp.at[here], xgot.at[mp], x_sem.at[0], x_sem.at[1], column(z))

    def each_z(body):
        def run(o, carry):
            step = (o + 1) // 2
            body(lax.rem(mp + jnp.where(lax.rem(o, 2) == 1, step, nz - step), nz))
            return carry

        lax.fori_loop(1, nz, run, 0)

    def each_peer(body):
        def run(o, carry):
            body(partner(o))
            return carry

        lax.fori_loop(1, groups, run, 0)

    xgot[mp] = xinp[pl.ds(pl.multiple_of(mp * chunk, chunk), chunk)]

    def r_copy(peer):
        return remote(rsend.at[peer], rgot.at[me], r_sem.at[0], r_sem.at[1], plane(peer))

    for step in range(4, half_ring - 1):
        uv_ring(step)
        if step == half_ring - 3:
            each_z(lambda z: x_copy(z).start())
    if half_ring < 7:
        each_z(lambda z: x_copy(z).start())

    def owner(k, carry):
        firsts = tenants_of(k, -1)

        @pl.when(k == 0)
        def _():
            drain(got, 2 * nd - 1, a_recv.at[0])

        @pl.when(k > 0)
        def _():
            drain(got, 2 * nd, a_recv.at[k])

        cots, crossed = [], []
        for first in firsts:
            for j in range(2):
                blk = got[first + j].astype(F32)
                cots.append(jnp.concatenate([blk[0:cap, 0:half_hid], blk[cap:, 0:half_hid]], axis=1))
                crossed.append(jnp.concatenate([blk[0:cap, half_hid:], blk[cap:, half_hid:]], axis=1))
        cots = jnp.concatenate(cots, axis=0).astype(BF16)
        at = pl.ds(pl.multiple_of(k * 2 * nd * cap, 2 * nd * cap), 2 * nd * cap)
        cotr[at] = cots
        crr[at] = jnp.concatenate(crossed, axis=0).astype(BF16)
        back = mm_nt(cots, wp[...])
        for j in range(2 * nd):
            s = slice(j * cap, (j + 1) * cap)
            rsend[firsts[j // 2] + j % 2] = jnp.concatenate(
                [back[s, 0:128], back[s, 128:WIDE]], axis=0
            ).astype(BF16)
        for first in firsts:
            for j in range(2):

                @pl.when(first + j != me)
                def _():
                    r_copy(first + j).start()

        return carry

    lax.fori_loop(0, nx, owner, 0)
    rgot[me] = rsend[me]
    if half_ring > 4:
        uv_ring(half_ring - 1)

    wgrad = mm_tn(crr[...], cotr[...])
    wg_out[...] = (wgrad[0:width] * scale).astype(BF16)
    stores = [
        pltpu.make_async_copy(wg_out, wg_hbm, out_sem.at[0]),
        pltpu.make_async_copy(uo.at[0], u_out_hbm, out_sem.at[1]),
        pltpu.make_async_copy(uo.at[1], v_out_hbm, out_sem.at[2]),
        pltpu.make_async_copy(bo, b_out_hbm, out_sem.at[3]),
        pltpu.make_async_copy(tab_out, tab_hbm, out_sem.at[4]),
    ]
    stores[0].start()

    drain(rgot, groups - 1, r_sem.at[1])

    def unpack(t, carry):
        pair = []
        for j in range(2):
            blk = rgot[2 * t + j].astype(F32)
            pair.append(jnp.concatenate([blk[0:cap], blk[cap:]], axis=1))
        backb[pl.ds(pl.multiple_of(t * 2 * cap, 2 * cap), 2 * cap)] = jnp.concatenate(
            pair, axis=0
        ).astype(BF16)
        return carry

    lax.fori_loop(0, groups // 2, unpack, 0)
    bh[...] = mm(perm_t[...], backb[...]).astype(BF16)

    def b_copy(z):
        here = pl.ds(pl.multiple_of(z * chunk, chunk), chunk)
        return remote(bh.at[here], bgot.at[mp], b_sem.at[0], b_sem.at[1], column(z))

    each_z(lambda z: b_copy(z).start())
    bgot[mp] = bh[pl.ds(pl.multiple_of(mp * chunk, chunk), chunk)]

    def piece_of(peer):
        return peer // per_half, pl.ds(pl.multiple_of(lax.rem(peer, per_half) * piece, piece), piece)

    def p_copy(i, peer):
        h, at = piece_of(peer)
        return remote(part.at[i, h, at], pgot.at[i, me], p_sem.at[i, 0], p_sem.at[i, 1], plane(peer))

    def q_copy(i, peer):
        h, at = piece_of(me)
        return remote(pred.at[i], pall.at[i, h, at], q_sem.at[i, 0], q_sem.at[i, 1], plane(peer))

    def scatter(i):
        each_peer(lambda p: p_copy(i, p).start())
        h, at = piece_of(me)
        pgot[i, me] = part[i, h, at]

    def gather(i):
        drain(pgot.at[i], groups - 1, p_sem.at[i, 1])
        pred[i] = (jnp.sum(pgot[i], axis=0) * scale).astype(BF16)
        each_peer(lambda p: q_copy(i, p).start())
        h, at = piece_of(me)
        pall[i, h, at] = pred[i]

    def gathered(i):
        drain(tally, (groups - 1) * piece, q_sem.at[i, 1])
        for h in range(2):
            uo[i, :, h * half_rank : (h + 1) * half_rank] = pall[i, h, 0:width].astype(F32)

    gate_h[...] = (bh[...].astype(F32) * xinp[...].astype(F32)).astype(BF16)
    u_part = mm_tn(gate_h[...], rank_ref[...])
    for h in range(2):
        part[0, h] = u_part[:, h * half_rank : (h + 1) * half_rank]
    part[0, 0, width : width + 8] = mm(jnp.ones((8, rows), BF16), gate_h[...])
    scatter(0)

    uv_ring(half_ring)
    for i in range(2):
        swap_copy(i).start()
    for z in range(nz):
        sib_copy(z).wait_recv()

    rank_here = rank_ref[pl.ds(pl.multiple_of(mp * chunk, chunk), chunk), :]

    def shift_of(z, carry):
        ends = uv[z, 0, 0, base:uv_rows].astype(F32)
        first = width - base
        bias_z = ends[first : first + 1] + ends[first + 1 : first + 2] + ends[first + 2 : first + 3]
        up = mm_nt(rank_here[:, 0:half_rank], uv[z, 0, 0]) + mm_nt(
            rank_here[:, half_rank:rank], uv[z, 1, 0]
        )
        shift[z] = up + bias_z + 1.0
        return carry

    lax.fori_loop(0, nz, shift_of, 0)
    for i in range(2):
        swap_copy(i).wait_recv()
        late_copy(i).start()
    gather(0)

    drain(xgot, nz - 1, x_sem.at[1])
    drain(bgot, nz - 1, b_sem.at[1])

    def rank_of(z, total):
        gate = (bgot[z].astype(F32) * xgot[z].astype(F32)).astype(BF16)
        return total[0] + mm(gate, uv[z, 0, 0]), total[1] + mm(gate, uv[z, 1, 0])

    zero = jnp.zeros((chunk, half_rank), F32)
    lo, up = lax.fori_loop(0, nz, rank_of, (zero, zero))
    rr = jnp.concatenate([lo, up], axis=1).astype(BF16)
    rr_all[mp] = rr

    def rr_copy(c, way, step, i):
        spot = rr_all.at[c, pl.ds(i * (chunk // 2), chunk // 2)]
        to = column(right if way == 0 else left)
        return remote(spot, spot, rr_send.at[i, way, step], rr_recv.at[i, c], to)

    for i in range(2):
        rr_copy(mp, 0, 0, i).start()
        rr_copy(mp, 1, 0, i).start()

    def rr_ring(step):
        came = lax.rem(mp + nz - step, nz)
        other = lax.rem(mp + step, nz)
        for i in range(2):
            rr_copy(came, 0, step - 1, i).wait_recv()
            if step < half_ring:
                rr_copy(came, 0, step, i).start()
                rr_copy(other, 1, step - 1, i).wait_recv()
            if step < half_ring - 1:
                rr_copy(other, 1, step, i).start()

    def input_of(z, carry):
        igp[z] = bgot[z].astype(F32) * shift[z] + (
            mm_nt(rr[:, 0:half_rank], uv[z, 0, 1]) + mm_nt(rr[:, half_rank:rank], uv[z, 1, 1])
        )
        return carry

    for i in range(2):
        late_copy(i).wait_recv()
    lax.fori_loop(0, nz // 2, input_of, 0)
    rr_ring(1)
    lax.fori_loop(nz // 2, nz, input_of, 0)
    rr_ring(2)
    igs[0] = jnp.zeros((chunk, EMB), BF16)
    for t in range(1, igs.shape[0]):
        pieces, at = [], t * EMB
        while at < (t + 1) * EMB:
            z, first = at // width, at % width
            stop = min(width, first + (t + 1) * EMB - at)
            pieces.append(igp[z][:, first:stop])
            at += stop - first
        igs[t] = jnp.concatenate(pieces, axis=1).astype(BF16)

    def t_copy(z):
        return remote(s5.at[z], tgot.at[mp], t_sem.at[0], t_sem.at[1], column(z))

    def fill(z, carry):
        for k in range(slots):
            s5[z, k] = igs[inv_ref[z * slots + k]]
        return carry

    lax.fori_loop(0, nz, fill, 0)
    sent = 0
    for step in range(3, half_ring + 1):
        rr_ring(step)
        upto = nz - 1 if step == half_ring else min(nz - 1, T_SENT[step - 3])
        for o in range(sent + 1, upto + 1):
            t_copy(lax.rem(mp + ((o + 1) // 2 if o % 2 else nz - o // 2), nz)).start()
        sent = upto
    tgot[mp] = s5[mp]

    v_part = mm(xin_t[...], rr_all[...].reshape(rows, rank))
    for h in range(2):
        part[1, h] = v_part[:, h * half_rank : (h + 1) * half_rank]
    scatter(1)
    gathered(0)
    bo[...] = pall[0, 0, width : width + 8].astype(F32)
    stores[1].start()
    stores[3].start()
    gather(1)

    drain(tgot, nz - 1, t_sem.at[1])
    for k in range(slots):
        values = tgot[:, k].reshape(rows, EMB)
        tab_out[k] = (mm(hot[k], values) * scale).astype(BF16)
    stores[4].start()
    gathered(1)
    stores[2].start()

    drain(send, groups - 1, a_send.at[0])
    drain(rsend, groups - 1, r_sem.at[0])
    drain(xgot, nz - 1, x_sem.at[0])
    drain(bgot, nz - 1, b_sem.at[0])
    drain(s5, nz - 1, t_sem.at[0])
    for i in range(2):
        drain(pgot.at[i], groups - 1, p_sem.at[i, 0])
        drain(tally, (groups - 1) * piece, q_sem.at[i, 0])
        swap_copy(i).wait_send()
        late_copy(i).wait_send()
    for z in range(nz):
        sib_copy(z).wait_send()
    for step in range(half_ring):
        uv_copy(mp, 0, step).wait_send()
        for i in range(2):
            rr_copy(mp, 0, step, i).wait_send()
        if step < half_ring - 1:
            uv_copy(mp, 1, step).wait_send()
            for i in range(2):
                rr_copy(mp, 1, step, i).wait_send()
    for store in stores:
        store.wait()


def hand_over(wg, u, v, b, table, wg_out, u_out, v_out, b_out, table_out, sems):
    pairs = [(wg, wg_out), (u, u_out), (v, v_out), (table, table_out)]
    copies = [pltpu.make_async_copy(a, c, sems.at[i]) for i, (a, c) in enumerate(pairs)]
    for copy in copies:
        copy.start()
    b_out[...] = b[0:1, 0 : b_out.shape[1]]
    for copy in copies:
        copy.wait()


def on_device(
    cross_in,
    rank_act,
    tower_cot,
    tenant_ids,
    sparse_ids,
    table_slot,
    cross_u,
    cross_v,
    cross_bias,
    tower_w,
):
    nd, nt, nz = lax.axis_size("dp"), lax.axis_size("tenant"), lax.axis_size("mp")
    groups = nd * nt
    rows, width = cross_in.shape
    rank, hid = rank_act.shape[1], tower_cot.shape[1]
    tables = table_slot.shape[0]
    slots = (tables + nz - 1) // nz
    cap = (5 * rows + 4 * groups - 1) // (4 * groups)
    chunk = rows // nz
    half_ring = nz // 2
    scale = 1.0 / math.sqrt(rows * groups)

    anywhere = pl.BlockSpec(memory_space=pl.ANY)
    smem = pl.BlockSpec(memory_space=pltpu.SMEM)
    sem = pltpu.SemaphoreType.DMA

    def bf(*shape):
        return pltpu.VMEM(shape, BF16)

    def ff(*shape):
        return pltpu.VMEM(shape, F32)

    out = pl.pallas_call(
        functools.partial(fused, nd, nt, nz, cap, scale),
        out_shape=(
            jax.ShapeDtypeStruct((width, hid), BF16),
            jax.ShapeDtypeStruct((width, rank), F32),
            jax.ShapeDtypeStruct((width, rank), F32),
            jax.ShapeDtypeStruct((8, WIDE), F32),
            jax.ShapeDtypeStruct((slots, VOCAB, EMB), BF16),
        ),
        in_specs=[smem] + [anywhere] * 9,
        out_specs=(anywhere,) * 5,
        scratch_shapes=[
            pltpu.VMEM((1, rows), jnp.int32),
            bf(width, rows),
            bf(width, rank),
            bf(rows, rank),
            ff(1, width),
            bf(rows, hid),
            bf(width, rank),
            bf(width, hid),
            pltpu.VMEM((tables, rows), jnp.int32),
            bf(width, hid),
            bf(slots, VOCAB, EMB),
            pltpu.SMEM((nz * slots,), jnp.int32),
            sem((9,)),
            sem((5,)),
            ff(2, width, rank),
            ff(8, WIDE),
            bf(nz, 2, 2, WIDE, rank // 2),
            bf(2, WIDE, rank // 2),
            bf(2, WIDE, rank // 2),
            bf(WIDE, rows),
            bf(rows, WIDE),
            bf(rows, WIDE),
            bf(WIDE, hid),
            pltpu.VMEM((8, rows), jnp.int32),
            bf(rows, groups * cap),
            bf(groups, 2 * cap, hid // 2 + 128),
            bf(groups, 2 * cap, hid // 2 + 128),
            bf(groups * cap, hid),
            bf(groups * cap, WIDE),
            bf(groups, 2 * cap, 128),
            bf(groups, 2 * cap, 128),
            bf(groups * cap, WIDE),
            bf(rows, WIDE),
            bf(rows, WIDE),
            bf(nz, chunk, WIDE),
            bf(nz, chunk, WIDE),
            ff(nz, chunk, WIDE),
            bf(nz, chunk, rank),
            ff(nz, chunk, WIDE),
            bf(tables + 1, chunk, EMB),
            bf(nz, slots, chunk, EMB),
            bf(nz, slots, chunk, EMB),
            bf(slots, VOCAB, rows),
            ff(2, 2, WIDE, WIDE),
            ff(2, groups, 2 * WIDE // groups, WIDE),
            bf(2, 2 * WIDE // groups, WIDE),
            bf(2, 2, WIDE, WIDE),
            bf((groups - 1) * 2 * WIDE // groups, WIDE),
            sem((2,)),
            sem((nt // 2,)),
            sem((2,)),
            sem((2,)),
            sem((2,)),
            sem((2, 2, half_ring)),
            sem((2, nz)),
            sem((2, nz)),
            sem((2, nz)),
            sem((2,)),
            sem((2,)),
            sem((2,)),
            sem((2,)),
            sem((2, 2, half_ring)),
            sem((2, nz)),
            sem((2,)),
            sem((2, 2)),
            sem((2, 2)),
        ],
        compiler_params=pltpu.CompilerParams(
            collective_id=0, has_side_effects=True, vmem_limit_bytes=60 * 2**20
        ),
    )(
        table_slot,
        tenant_ids.T,
        cross_in.T,
        cross_u,
        rank_act,
        cross_bias[None, :],
        tower_cot,
        cross_v,
        tower_w[0],
        sparse_ids.T,
    )
    vmem = pl.BlockSpec(memory_space=pltpu.VMEM)
    wgrad, u_total, v_total, b_total, table = pl.pallas_call(
        hand_over,
        out_shape=tuple(
            jax.ShapeDtypeStruct((1, width) if i == 3 else x.shape, x.dtype)
            for i, x in enumerate(out)
        ),
        in_specs=[vmem] * 5,
        out_specs=(anywhere, anywhere, anywhere, vmem, anywhere),
        scratch_shapes=[sem((4,))],
    )(*out)
    return wgrad[None], u_total, v_total, b_total[0], table[None]


def solution(mesh):
    return jax.shard_map(
        on_device,
        mesh=mesh,
        in_specs=(
            P(("dp", "tenant"), "mp"),
            P(("dp", "tenant"), None),
            P(("dp", "tenant"), None),
            P(("dp", "tenant"), None),
            P(("dp", "tenant"), None),
            P(),
            P("mp", None),
            P("mp", None),
            P("mp"),
            P(("dp", "tenant"), "mp", None),
        ),
        out_specs=(
            P(("dp", "tenant"), "mp", None),
            P("mp", None),
            P("mp", None),
            P("mp"),
            P(("dp", "tenant"), "mp", None, None),
        ),
        check_vma=False,
    )
```
